128 devices in a mesh: section: 4 (over y), bar: 32 (over x, z, core).
Axes of the slice: x: 4, y: 4, z: 4, core: 2. Of those that a mesh axis runs over, the one named last changes fastest.
Arguments:
- bar_in: bfloat16 [4, 128, 4096], P(None, None, 'bar'), may hold values from -6 to 6
- section_weight: bfloat16 [4, 4096, 4096], P('section', None, 'bar'), may hold values from -0.09375 to 0.09375
- section_gain: float32 [4, 4096], P('section'), may hold values from 0.1 to 1.9
- projection: bfloat16 [4096, 1024], P('bar'), may hold values from -0.09375 to 0.09375
- char_ids: int32 [4, 128, 128], P('section', 'bar'), may hold values from 0 to 127
- lengths: int32 [4, 128], P('section', 'bar'), may hold values from 1 to 128
- char_embed: bfloat16 [128, 1024], replicated, may hold values from -4 to 4
- char_pos: bfloat16 [128, 1024], replicated, may hold values from -3 to 3
- attn_in: bfloat16 [1024, 3072], P(('section', 'bar')), may hold values from -2 to 2
- attn_out: bfloat16 [1024, 1024], P(('section', 'bar')), may hold values from -0.1875 to 0.1875
- ffn_in: bfloat16 [1024, 4096], P(('section', 'bar')), may hold values from -0.1875 to 0.1875
- ffn_out: bfloat16 [4096, 1024], P(('section', 'bar')), may hold values from -0.09375 to 0.09375
- norm_gain: float32 [3, 1024], replicated, may hold values from 0.1 to 1.9
Outputs:
- char_logp: float32 [4, 128, 128], P('section', 'bar')
The draws below stay inside these ranges and needn't reach their ends.
All inputs are finite; a program needn't handle non-finite values.
Results may differ from the reference program's by a relative error of at most 0.0009.
Values may be sent and summed in bfloat16 or wider, within the bound.
No kernel may reach another device: no remote copies, remote signals or barrier semaphores. Data moves between devices by JAX's collectives and lax.ppermute only.
A program may use at most 128 MiB of HBM per device.

```python
import jax
import jax.numpy as jnp
from jax import lax

D = 4096
CD = 1024
CHEADS = 16
CHD = 64
FF = 4096
VOCAB = 128
CHARS = 128
MICRO = 4
BARS = 128
N_SECTION = 4


def draw_attn_in(key, part):
    key = jax.random.fold_in(key, 7)
    baseline_key = jax.random.fold_in(key, 1)
    planting_key = jax.random.fold_in(key, 2)
    heads_key = jax.random.fold_in(key, 3)
    baseline = jnp.clip(jax.random.normal(baseline_key, (CD, 3 * CD), jnp.float32), -6.0, 6.0) * CD ** (-0.5)
    planting = jnp.clip(jax.random.normal(planting_key, (CD, CD), jnp.float32), -3.0, 3.0) * CD ** (-0.5)
    head_rank = jax.random.permutation(heads_key, CHEADS)
    second_scale = 3.5 if CHEADS >= 8 else 0.0
    head_scale = jnp.where(head_rank == 0, 6.0, jnp.where(head_rank == 1, second_scale, 0.0)).astype(jnp.float32)
    column_scale = jnp.repeat(head_scale, CHD)
    planted = column_scale > 0.0
    planted_cols = column_scale[None, :] * planting
    queries = jnp.where(planted[None, :], planted_cols, baseline[:, :CD])
    keys_part = jnp.where(planted[None, :], planted_cols, baseline[:, CD:2 * CD])
    joined = jnp.concatenate([queries, keys_part, baseline[:, 2 * CD:]], axis=1)
    return joined.astype(jnp.bfloat16)


def with_ends(drawn, rng, least, largest):
    index_at = [jax.random.randint(jax.random.fold_in(rng, axis), (), 0, length) for axis, length in enumerate(drawn.shape)]
    main_axis = drawn.shape.index(max(drawn.shape))
    beside = index_at[:main_axis] + [(index_at[main_axis] + 1) % drawn.shape[main_axis]] + index_at[main_axis + 1:]
    return drawn.at[tuple(index_at)].set(least).at[tuple(beside)].set(largest)


def level_of(key, dims, split, low, largest):
    def one(dim, shards_of):
        steps = jax.random.uniform(jax.random.fold_in(jax.random.fold_in(key, 6), dim), (shards_of,), jnp.float32, low / len(split), largest / len(split))
        return jnp.repeat(jnp.exp(steps), dims[dim] // shards_of).reshape((-1,) + (1,) * (len(dims) - dim - 1))

    level = one(*split[0])
    for cut in split[1:]:
        level = level * one(*cut)
    return level


def normal_values(own_key, dims, width, bound, cuts=(), kind=jnp.bfloat16):
    loudness = level_of(own_key, dims, cuts, -0.22, 0.18) if cuts else 1.0
    drawn = jax.random.normal(own_key, dims, jnp.float32) * width * loudness
    return jnp.minimum(jnp.maximum(drawn, -bound), bound).astype(kind)


def setup_inputs(seed: int = 0) -> dict:
    key_of = jax.random.split(jax.random.key(seed), 14)
    bar_in = normal_values(key_of[0], (MICRO, BARS, D), 1.0, 6.0, ((2, 32),))
    section_weight = normal_values(key_of[1], (N_SECTION, D, D), D ** -0.5, 0.09375, ((0, 4), (2, 32)))
    section_gain = jnp.clip(1.0 + 0.18 * jax.random.normal(key_of[2], (N_SECTION, D), jnp.float32), 0.1, 1.9)
    projection = normal_values(key_of[3], (D, CD), D ** -0.5, 0.09375, ((0, 32),))
    char_ids = with_ends(jax.random.randint(key_of[4], (MICRO, BARS, CHARS), 0, VOCAB), jax.random.fold_in(key_of[4], 1), 0, VOCAB - 1).astype(jnp.int32)
    lengths = with_ends(jax.random.randint(key_of[5], (MICRO, BARS), 1, CHARS + 1), jax.random.fold_in(key_of[5], 1), 1, CHARS).astype(jnp.int32)
    char_embed = normal_values(key_of[6], (VOCAB, CD), 0.7, 4.0)
    char_pos = normal_values(key_of[7], (CHARS, CD), 0.5, 3.0)
    attn_in = draw_attn_in(jax.random.fold_in(key_of[13], 71), 0)
    attn_out = normal_values(key_of[9], (CD, CD), CD ** -0.5, 0.1875, ((0, 128),))
    ffn_in = normal_values(key_of[10], (CD, FF), CD ** -0.5, 0.1875, ((0, 128),))
    ffn_out = normal_values(key_of[11], (FF, CD), FF ** -0.5, 0.09375, ((0, 128),))
    norm_gain = jnp.clip(1.0 + 0.18 * jax.random.normal(key_of[12], (3, CD), jnp.float32), 0.1, 1.9)
    return {"bar_in": bar_in, "section_weight": section_weight, "section_gain": section_gain, "projection": projection, "char_ids": char_ids, "lengths": lengths, "char_embed": char_embed, "char_pos": char_pos, "attn_in": attn_in, "attn_out": attn_out, "ffn_in": ffn_in, "ffn_out": ffn_out, "norm_gain": norm_gain}


def rms_scale(values, gain_row):
    return values * lax.rsqrt(lax.optimization_barrier(jnp.mean(values * values, axis=-1, keepdims=True)) + 1e-05) * gain_row

def char_decoder(bar_vectors, char_ids, lengths, char_embed, char_pos, attn_in, attn_out, ffn_in, ffn_out, norm_gain):
    bar_count = bar_vectors.shape[0]
    char_count = char_ids.shape[1]
    vocab_size = char_embed.shape[0]
    model_width = char_embed.shape[1]
    head_count = model_width // CHD
    earlier = jax.nn.one_hot(char_ids[:, :-1].reshape(-1), vocab_size, dtype=jnp.bfloat16)
    embedded = jnp.dot(earlier, char_embed, preferred_element_type=jnp.float32).reshape(bar_count, char_count - 1, model_width)
    inputs = jnp.concatenate([bar_vectors.astype(jnp.float32)[:, None, :], embedded], axis=1)
    inputs = (inputs + char_pos.astype(jnp.float32)[None]).reshape(bar_count * char_count, model_width)
    normed = rms_scale(inputs, norm_gain[0]).astype(jnp.bfloat16)
    project = jnp.dot(normed, attn_in, preferred_element_type=jnp.float32).astype(jnp.bfloat16)
    project = project.reshape(bar_count, char_count, 3, head_count, CHD).astype(jnp.float32)
    queries = project[:, :, 0]
    keys_all = project[:, :, 1]
    values = project[:, :, 2]
    scores = jnp.einsum('bqhd,bkhd->bhqk', queries, keys_all) * CHD ** (-0.5)
    position = jnp.arange(char_count)
    causal = position[None, :] <= position[:, None]
    scores = jnp.where(causal[None, None], scores, -1e+30)
    weights = jax.nn.softmax(scores, axis=-1).astype(jnp.bfloat16)
    context = jnp.einsum('bhqk,bkhd->bqhd', weights.astype(jnp.float32), values).astype(jnp.bfloat16)
    context = context.reshape(bar_count * char_count, model_width)
    hidden = inputs + jnp.dot(context, attn_out, preferred_element_type=jnp.float32)
    normed = rms_scale(hidden, norm_gain[1]).astype(jnp.bfloat16)
    middle = jax.nn.gelu(jnp.dot(normed, ffn_in, preferred_element_type=jnp.float32)).astype(jnp.bfloat16)
    hidden = hidden + jnp.dot(middle, ffn_out, preferred_element_type=jnp.float32)
    normed = rms_scale(hidden, norm_gain[2]).astype(jnp.bfloat16)
    logits = jnp.dot(normed, char_embed.T, preferred_element_type=jnp.float32)
    logprob = logits - jax.nn.logsumexp(logits, axis=-1, keepdims=True)
    picker = jax.nn.one_hot(char_ids.reshape(-1), vocab_size, dtype=jnp.float32)
    chosen = lax.optimization_barrier(jnp.sum(picker * logprob, axis=-1)).reshape(bar_count, char_count)
    live_mask = position[None, :] < lengths[:, None]
    return jnp.where(live_mask, chosen, 0.0)

def reference(bar_in, section_weight, section_gain, projection, char_ids, lengths, char_embed, char_pos, attn_in, attn_out, ffn_in, ffn_out, norm_gain):
    results = []
    for micro_index in range(MICRO):
        bar_rows = bar_in[micro_index]
        for section_step in range(N_SECTION):
            normed = rms_scale(bar_rows.astype(jnp.float32), section_gain[section_step]).astype(jnp.bfloat16)
            update = jax.nn.gelu(jnp.dot(normed, section_weight[section_step], preferred_element_type=jnp.float32))
            bar_rows = (bar_rows.astype(jnp.float32) + update).astype(jnp.bfloat16)
        vectors = jnp.dot(bar_rows, projection, preferred_element_type=jnp.float32).astype(jnp.bfloat16)
        results.append(char_decoder(vectors, char_ids[micro_index], lengths[micro_index], char_embed, char_pos, attn_in, attn_out, ffn_in, ffn_out, norm_gain))
    return jnp.stack(results)
```

```python
import jax, jax.numpy as jnp
from jax import lax
from jax.sharding import PartitionSpec as P
from jax.experimental import pallas as pl
from jax.experimental.pallas import tpu as pltpu

BF=jnp.bfloat16
F32=jnp.float32

def rms_rows(v, g):
    return v * lax.rsqrt(jnp.mean(v * v, axis=-1, keepdims=True) + 1e-05) * g


def char_kernel(parts_ref, ids_ref, prev_ref, len_ref, embed_ref, pos_ref, gain_ref, pack_ref, out_ref,
                x_ref, n_ref, q_ref, k_ref, v_ref, c_ref, mid_ref, wq, wup, wdn, sems):
    bars, chars = ids_ref.shape
    width = embed_ref.shape[1]
    copies = []
    for j in range(4):
        copies.append(pltpu.make_async_copy(pack_ref.at[:, j], wq.at[j], sems.at[j]))
    for j in range(4):
        copies.append(pltpu.make_async_copy(pack_ref.at[:, 4 + j], wup.at[j], sems.at[4 + j]))
    for j in range(4):
        rows = pl.ds(32 * j, 32)
        copies.append(pltpu.make_async_copy(pack_ref.at[rows, 8:12], wdn.at[rows], sems.at[8 + j]))
    for i in (0, 1, 2, 3, 4, 8, 5, 9, 6, 10, 7, 11):
        copies[i].start()
    vocab = embed_ref.shape[0]
    vec = jnp.sum(parts_ref[...], axis=0).astype(BF).astype(F32)
    row_id = lax.broadcasted_iota(jnp.int32, (chars, width), 0)
    for b in range(bars):
        one_hot = (lax.broadcasted_iota(jnp.int32, (vocab, chars), 0) == prev_ref[b:b + 1, :]).astype(BF)
        emb = lax.dot_general(one_hot, embed_ref[...], (((0,), (0,)), ((), ())), preferred_element_type=F32)
        emb = jnp.where(row_id == 0, vec[b:b + 1], emb) + pos_ref[...].astype(F32)
        x_ref[b * chars:(b + 1) * chars] = emb
        n_ref[b * chars:(b + 1) * chars] = rms_rows(emb, gain_ref[0:1]).astype(BF)
    for j, dst in ((0, q_ref), (1, k_ref), (2, v_ref)):
        copies[j].wait()
        dst[...] = jnp.dot(n_ref[...], wq[j].reshape(width, width), preferred_element_type=F32).astype(BF)

    lane = lax.broadcasted_iota(jnp.int32, (chars, 128), 1)
    low = lane < 64
    causal = lax.broadcasted_iota(jnp.int32, (chars, chars), 0) >= lax.broadcasted_iota(jnp.int32, (chars, chars), 1)

    def attend(b, carry):
        rows = pl.ds(pl.multiple_of(b * chars, chars), chars)
        for h in range(width // 128):
            cols = slice(h * 128, (h + 1) * 128)
            q, k, v = q_ref[rows, cols], k_ref[rows, cols], v_ref[rows, cols]
            zero = jnp.zeros_like(k)
            kk = jnp.concatenate([jnp.where(low, k, zero), jnp.where(low, zero, k)], axis=0)
            vv = jnp.concatenate([jnp.where(low, v, zero), jnp.where(low, zero, v)], axis=0)
            s = lax.dot_general(q, kk, (((1,), (1,)), ((), ())), preferred_element_type=F32)
            probs = []
            for half in range(2):
                t = jnp.where(causal, s[:, half * chars:(half + 1) * chars], -1e30)
                e = jnp.exp((t - jnp.max(t, axis=-1, keepdims=True)) * 0.125)
                probs.append((e * (1.0 / jnp.sum(e, axis=-1, keepdims=True))).astype(BF))
            c_ref[rows, cols] = jnp.dot(jnp.concatenate(probs, axis=1), vv, preferred_element_type=F32).astype(BF)
        return carry

    lax.fori_loop(0, bars, attend, 0)
    copies[3].wait()
    hidden = x_ref[...] + jnp.dot(c_ref[...], wq[3].reshape(width, width), preferred_element_type=F32)
    x_ref[...] = hidden
    n_ref[...] = rms_rows(hidden, gain_ref[1:2]).astype(BF)
    for j in range(4):
        copies[4 + j].wait()
        mid_ref[...] = jax.nn.gelu(jnp.dot(n_ref[...], wup[j].reshape(width, width), preferred_element_type=F32)).astype(BF)
        copies[8 + j].wait()
        x_ref[...] += jnp.dot(mid_ref[...], wdn[32 * j:32 * j + 32].reshape(width, width), preferred_element_type=F32)
    last = rms_rows(x_ref[...], gain_ref[2:3]).astype(BF)
    logits = lax.dot_general(embed_ref[...], last, (((1,), (1,)), ((), ())), preferred_element_type=F32)
    top = jnp.max(logits, axis=0, keepdims=True)
    norm = top + jnp.log(jnp.sum(jnp.exp(logits - top), axis=0, keepdims=True))
    for b in range(bars):
        cols = slice(b * chars, (b + 1) * chars)
        hit = lax.broadcasted_iota(jnp.int32, (vocab, chars), 0) == ids_ref[b:b + 1, :]
        picked = jnp.sum(jnp.where(hit, logits[:, cols], 0.0), axis=0, keepdims=True) - norm[:, cols]
        live = lax.broadcasted_iota(jnp.int32, (1, chars), 1) < len_ref[b:b + 1, :]
        out_ref[b:b + 1, :] = jnp.where(live, picked, 0.0)


def char_decode(parts, ids, lengths, embed, pos, gain, pack):
    bars, chars = ids.shape
    width = embed.shape[1]
    tokens = bars * chars
    prev = jnp.concatenate([jnp.full((bars, 1), -1, jnp.int32), ids[:, :-1]], axis=1)
    vm = pl.BlockSpec(memory_space=pltpu.VMEM)
    t = lambda d: pltpu.VMEM((tokens, width), d)
    return pl.pallas_call(
        char_kernel,
        out_shape=jax.ShapeDtypeStruct((bars, chars), F32),
        in_specs=[vm] * 7 + [pl.BlockSpec(memory_space=pl.ANY)],
        out_specs=vm,
        scratch_shapes=[t(F32), t(BF), t(BF), t(BF), t(BF), t(BF), t(BF),
                        pltpu.VMEM((4, 128, 8, width), BF), pltpu.VMEM((4, 128, 8, width), BF),
                        pltpu.VMEM((128, 4, 8, width), BF), pltpu.SemaphoreType.DMA((12,))],
        compiler_params=pltpu.CompilerParams(vmem_limit_bytes=56 << 20),
        name="char_decode",
    )(parts, ids, prev, lengths[:, None], embed, pos, gain, pack)


GROUP = ("y", "x", "z", "c")


def section_kernel(copies, project, where_ref, x_ref, gain_ref, *refs):
    own, other = refs[:copies], refs[copies:2 * copies]
    refs = refs[2 * copies:]
    if project:
        proj_ref, refs = refs[0], refs[1:]
    out_ref, n_ref, w_ref, sems = refs
    blocks, rows, cols = x_ref.shape
    half = cols // 2
    which, core, chip = where_ref[0], where_ref[1], where_ref[2]
    first = pl.ds(pl.multiple_of(core * half, half), half)
    second = pl.ds(pl.multiple_of((1 - core) * half, half), half)
    for i in range(copies):
        @pl.when(which == i)
        def _():
            pltpu.make_async_copy(own[i], w_ref.at[:, first], sems.at[0]).start()
            pltpu.make_async_copy(other[i], w_ref.at[:, second], sems.at[1]).start()
    total = jnp.zeros((rows, cols), F32)
    for j in range(blocks):
        v = x_ref[j].astype(F32)
        total += v * v
    scale = lax.rsqrt(jnp.sum(total, axis=-1, keepdims=True) / (blocks * cols) + 1e-05)
    gain = gain_ref[which]
    for j in range(blocks):
        span = slice(j * cols, (j + 1) * cols)
        n_ref[:, span] = (x_ref[j].astype(F32) * scale * gain[:, span]).astype(BF)
    pltpu.make_async_copy(own[0], w_ref.at[:, first], sems.at[0]).wait()
    pltpu.make_async_copy(other[0], w_ref.at[:, second], sems.at[1]).wait()
    update = jax.nn.gelu(jnp.dot(n_ref[...], w_ref[...], preferred_element_type=F32))
    leaving = (x_ref[chip].astype(F32) + update).astype(BF)
    if project:
        partial = jnp.dot(leaving, proj_ref[...], preferred_element_type=F32)
        each = rows // blocks
        for j in range(blocks):
            out_ref[j] = partial[j * each:(j + 1) * each]
    else:
        each = out_ref.shape[1]
        for j in range(out_ref.shape[0]):
            out_ref[j] = leaving if each == rows else leaving[j * each:(j + 1) * each]


def section_step(where, x, gain, own, other, out_shape, proj=None):
    blocks, rows, cols = x.shape
    depth = blocks * cols
    vm = pl.BlockSpec(memory_space=pltpu.VMEM)
    hbm = pl.BlockSpec(memory_space=pl.ANY)
    extra = [] if proj is None else [proj]
    return pl.pallas_call(
        lambda *refs: section_kernel(len(own), proj is not None, *refs),
        out_shape=out_shape,
        in_specs=[pl.BlockSpec(memory_space=pltpu.SMEM), vm, vm] + [hbm] * (2 * len(own)) + [vm] * len(extra),
        out_specs=vm,
        scratch_shapes=[pltpu.VMEM((rows, depth), BF), pltpu.VMEM((depth, cols), BF), pltpu.SemaphoreType.DMA((2,))],
        compiler_params=pltpu.CompilerParams(vmem_limit_bytes=32 << 20),
        name="section",
    )(where, x, gain, *own, *other, *extra)


def body(bar_in, section_weight, section_gain, projection, char_ids, lengths, char_embed, char_pos,
         attn_in, attn_out, ffn_in, ffn_out, norm_gain):
    y, core = lax.axis_index("y"), lax.axis_index("c")
    chip = lax.axis_index("x") * 4 + lax.axis_index("z")
    width = char_embed.shape[1]

    def swap(v):
        return lax.ppermute(v, "c", [(0, 1), (1, 0)])

    def turn(v, by):
        return lax.ppermute(v, "y", [(i, (i + by) % 4) for i in range(4)])

    def ordered(mine, theirs, axis):
        return jnp.where(core == 0, jnp.concatenate([mine, theirs], axis), jnp.concatenate([theirs, mine], axis))

    def spread(v):
        return lax.all_to_all(v, ("x", "z"), 0, 0, tiled=True)

    pack = jnp.concatenate(
        [attn_in[:, i * width:(i + 1) * width] for i in range(3)] + [attn_out]
        + [ffn_in[:, i * width:(i + 1) * width] for i in range(4)] + [ffn_out], axis=0)
    pack = lax.all_gather(pack, GROUP, axis=0, tiled=True).reshape(128, 12, 8, width)

    own = [section_weight[0]]
    gains = [section_gain]
    for by in (1, 2, 3):
        own.append(turn(section_weight[0], by))
        gains.append(turn(section_gain, by))
    other = [swap(w) for w in own]
    proj = ordered(projection, swap(projection), 0)

    micro, bars, feats = bar_in.shape
    by_core = bar_in.reshape(micro, 16, 2, 4, feats).transpose(2, 0, 1, 3, 4).reshape(2, micro * 64, feats)
    mine = lax.dynamic_index_in_dim(by_core, core, 0, keepdims=False)
    theirs = swap(lax.dynamic_index_in_dim(by_core, 1 - core, 0, keepdims=False))
    block = ordered(mine, theirs, 1)
    x = spread(jnp.broadcast_to(block[None], (16,) + block.shape))

    def where(step):
        return jnp.stack([lax.rem(y - step + 4, 4) if step else jnp.int32(0), core, chip])

    first = section_step(where(0), x, section_gain[None], own[:1], other[:1],
                         jax.ShapeDtypeStruct((micro, 64, 2 * feats), BF))
    rows = lax.all_to_all(first, "y", 0, 0, tiled=True)[0]
    out = jnp.broadcast_to(rows[None], (16,) + rows.shape)
    gain = jnp.stack(gains)
    for step in (1, 2, 3):
        x = spread(out)
        shape = jax.ShapeDtypeStruct((16, 64, 2 * feats), BF) if step < 3 else jax.ShapeDtypeStruct((16, 4, width), F32)
        out = section_step(where(step), x, gain, own, other, shape, proj if step == 3 else None)
    parts = spread(out)
    return char_decode(parts, char_ids[0], lengths[0], char_embed, char_pos, norm_gain, pack)[None]


def solution(mesh):
    fine = jax.sharding.Mesh(mesh.devices.reshape(4, 4, 4, 2), GROUP)
    bar = ("x", "z", "c")
    in_specs = (
        P(None, None, bar),
        P("y", None, bar),
        P("y", None),
        P(bar, None),
        P("y", bar, None),
        P("y", bar),
        P(),
        P(),
        P(GROUP, None),
        P(GROUP, None),
        P(GROUP, None),
        P(GROUP, None),
        P(),
    )
    return jax.shard_map(body, mesh=fine, in_specs=in_specs, out_specs=P("y", bar, None), check_vma=False)
```

```python
import jax, jax.numpy as jnp
from jax import lax
from jax.sharding import PartitionSpec as P
from jax.experimental import pallas as pl
from jax.experimental.pallas import tpu as pltpu

BF=jnp.bfloat16
F32=jnp.float32

def rms_rows(v, g):
    return v * lax.rsqrt(jnp.mean(v * v, axis=-1, keepdims=True) + 1e-05) * g


def char_kernel(parts_ref, ids_ref, prev_ref, len_ref, embed_ref, pos_ref, gain_ref, pack_ref, out_ref,
                x_ref, n_ref, q_ref, k_ref, v_ref, c_ref, mid_ref, wq, wup, wdn, sems):
    bars, chars = ids_ref.shape
    width = embed_ref.shape[1]
    copies = []
    for j in range(4):
        copies.append(pltpu.make_async_copy(pack_ref.at[:, j], wq.at[j], sems.at[j]))
    for j in range(4):
        copies.append(pltpu.make_async_copy(pack_ref.at[:, 4 + j], wup.at[j], sems.at[4 + j]))
    for j in range(4):
        rows = pl.ds(32 * j, 32)
        copies.append(pltpu.make_async_copy(pack_ref.at[rows, 8:12], wdn.at[rows], sems.at[8 + j]))
    for i in (0, 1, 2, 3, 4, 8, 5, 9, 6, 10, 7, 11):
        copies[i].start()
    vocab = embed_ref.shape[0]
    vec = jnp.sum(parts_ref[...], axis=0).astype(BF).astype(F32)
    row_id = lax.broadcasted_iota(jnp.int32, (chars, width), 0)
    for b in range(bars):
        one_hot = (lax.broadcasted_iota(jnp.int32, (vocab, chars), 0) == prev_ref[b:b + 1, :]).astype(BF)
        emb = lax.dot_general(one_hot, embed_ref[...], (((0,), (0,)), ((), ())), preferred_element_type=F32)
        emb = jnp.where(row_id == 0, vec[b:b + 1], emb) + pos_ref[...].astype(F32)
        x_ref[b * chars:(b + 1) * chars] = emb
        n_ref[b * chars:(b + 1) * chars] = rms_rows(emb, gain_ref[0:1]).astype(BF)
    for j, dst in ((0, q_ref), (1, k_ref), (2, v_ref)):
        copies[j].wait()
        dst[...] = jnp.dot(n_ref[...], wq[j].reshape(width, width), preferred_element_type=F32).astype(BF)

    lane = lax.broadcasted_iota(jnp.int32, (chars, 128), 1)
    low = lane < 64
    causal = lax.broadcasted_iota(jnp.int32, (chars, chars), 0) >= lax.broadcasted_iota(jnp.int32, (chars, chars), 1)

    def attend(b, carry):
        rows = pl.ds(pl.multiple_of(b * chars, chars), chars)
        for h in range(width // 128):
            cols = slice(h * 128, (h + 1) * 128)
            q, k, v = q_ref[rows, cols], k_ref[rows, cols], v_ref[rows, cols]
            zero = jnp.zeros_like(k)
            kk = jnp.concatenate([jnp.where(low, k, zero), jnp.where(low, zero, k)], axis=0)
            vv = jnp.concatenate([jnp.where(low, v, zero), jnp.where(low, zero, v)], axis=0)
            s = lax.dot_general(q, kk, (((1,), (1,)), ((), ())), preferred_element_type=F32)
            probs = []
            for half in range(2):
                t = jnp.where(causal, s[:, half * chars:(half + 1) * chars], -1e30)
                e = jnp.exp((t - jnp.max(t, axis=-1, keepdims=True)) * 0.125)
                probs.append((e * (1.0 / jnp.sum(e, axis=-1, keepdims=True))).astype(BF))
            c_ref[rows, cols] = jnp.dot(jnp.concatenate(probs, axis=1), vv, preferred_element_type=F32).astype(BF)
        return carry

    lax.fori_loop(0, bars, attend, 0)
    copies[3].wait()
    hidden = x_ref[...] + jnp.dot(c_ref[...], wq[3].reshape(width, width), preferred_element_type=F32)
    x_ref[...] = hidden
    n_ref[...] = rms_rows(hidden, gain_ref[1:2]).astype(BF)
    for j in range(4):
        copies[4 + j].wait()
        mid_ref[...] = jax.nn.gelu(jnp.dot(n_ref[...], wup[j].reshape(width, width), preferred_element_type=F32)).astype(BF)
        copies[8 + j].wait()
        x_ref[...] += jnp.dot(mid_ref[...], wdn[32 * j:32 * j + 32].reshape(width, width), preferred_element_type=F32)
    last = rms_rows(x_ref[...], gain_ref[2:3]).astype(BF)
    logits = lax.dot_general(embed_ref[...], last, (((1,), (1,)), ((), ())), preferred_element_type=F32)
    top = jnp.max(logits, axis=0, keepdims=True)
    norm = top + jnp.log(jnp.sum(jnp.exp(logits - top), axis=0, keepdims=True))
    for b in range(bars):
        cols = slice(b * chars, (b + 1) * chars)
        hit = lax.broadcasted_iota(jnp.int32, (vocab, chars), 0) == ids_ref[b:b + 1, :]
        picked = jnp.sum(jnp.where(hit, logits[:, cols], 0.0), axis=0, keepdims=True) - norm[:, cols]
        live = lax.broadcasted_iota(jnp.int32, (1, chars), 1) < len_ref[b:b + 1, :]
        out_ref[b:b + 1, :] = jnp.where(live, picked, 0.0)


def char_decode(parts, ids, lengths, embed, pos, gain, pack):
    bars, chars = ids.shape
    width = embed.shape[1]
    tokens = bars * chars
    prev = jnp.concatenate([jnp.full((bars, 1), -1, jnp.int32), ids[:, :-1]], axis=1)
    vm = pl.BlockSpec(memory_space=pltpu.VMEM)
    t = lambda d: pltpu.VMEM((tokens, width), d)
    return pl.pallas_call(
        char_kernel,
        out_shape=jax.ShapeDtypeStruct((bars, chars), F32),
        in_specs=[vm] * 7 + [pl.BlockSpec(memory_space=pl.ANY)],
        out_specs=vm,
        scratch_shapes=[t(F32), t(BF), t(BF), t(BF), t(BF), t(BF), t(BF),
                        pltpu.VMEM((4, 128, 8, width), BF), pltpu.VMEM((4, 128, 8, width), BF),
                        pltpu.VMEM((128, 4, 8, width), BF), pltpu.SemaphoreType.DMA((12,))],
        compiler_params=pltpu.CompilerParams(vmem_limit_bytes=56 << 20),
        name="char_decode",
    )(parts, ids, prev, lengths[:, None], embed, pos, gain, pack)


GROUP = ("y", "x", "z", "c")


def section_kernel(project, where_ref, x_ref, *refs):
    own, other, refs = refs[:4], refs[4:8], refs[8:]
    if project:
        proj_own, proj_other, out_ref, w_ref, sems, p_ref, p_sems = refs
    else:
        out_ref, w_ref, sems, row_ref, out_sems = refs
    blocks, rows, cols = x_ref.shape
    side, depth = cols // 2, blocks * cols
    half = depth // 2
    which, core, chip = where_ref[0], where_ref[1], where_ref[2]
    for i in range(4):
        @pl.when(which == i)
        def _():
            for sources, at, sem in ((own, core, 0), (other, 1 - core, 1)):
                lanes = pl.ds(pl.multiple_of(at * side, side), side)
                for part in range(2):
                    span = pl.ds(part * half, half)
                    pltpu.make_async_copy(
                        sources[i].at[span], w_ref.at[span, lanes], sems.at[2 * sem + part]
                    ).start()
    if project:
        deep = proj_own.shape[0]
        loads = [
            pltpu.make_async_copy(source, p_ref.at[pl.ds(pl.multiple_of(at * deep, deep), deep)], p_sems.at[i])
            for i, (source, at) in enumerate(((proj_own, core), (proj_other, 1 - core)))
        ]
        for load in loads:
            load.start()
    total = jnp.zeros((rows, cols), F32)
    for j in range(blocks):
        v = x_ref[j].astype(F32)
        total += v * v
    scale = lax.rsqrt(jnp.sum(total, axis=-1, keepdims=True) / depth + 1e-05)
    for i in range(4):
        span = pl.ds(i % 2 * half, half)
        pltpu.make_async_copy(own[0].at[span], w_ref.at[span, pl.ds(i // 2 * side, side)], sems.at[i]).wait()
    wide = jnp.concatenate([x_ref[j] for j in range(blocks)], axis=1)
    update = jax.nn.gelu(jnp.dot(wide, w_ref[...], preferred_element_type=F32) * scale)
    leaving = (x_ref[chip].astype(F32) + update).astype(BF)
    if project:
        for load in loads:
            load.wait()
        partial = jnp.dot(leaving, p_ref[...], preferred_element_type=F32)
        each = rows // blocks
        for j in range(blocks):
            out_ref[j] = partial[j * each:(j + 1) * each]
    else:
        row_ref[...] = leaving
        sends = [pltpu.make_async_copy(row_ref, out_ref.at[j], out_sems.at[j]) for j in range(blocks)]
        for send in sends:
            send.start()
        for send in sends:
            send.wait()


def section_step(where, x, own, other, proj=None):
    blocks, rows, cols = x.shape
    vm = pl.BlockSpec(memory_space=pltpu.VMEM)
    hbm = pl.BlockSpec(memory_space=pl.ANY)
    scratch = [pltpu.VMEM((blocks * cols, cols), BF), pltpu.SemaphoreType.DMA((4,))]
    if proj is None:
        proj, out, out_spec = [], jax.ShapeDtypeStruct(x.shape, BF), hbm
        scratch += [pltpu.VMEM((rows, cols), BF), pltpu.SemaphoreType.DMA((blocks,))]
    else:
        width = proj[0].shape[1]
        out, out_spec = jax.ShapeDtypeStruct((blocks, rows // blocks, width), F32), vm
        scratch += [pltpu.VMEM((cols, width), BF), pltpu.SemaphoreType.DMA((2,))]
    return pl.pallas_call(
        lambda *refs: section_kernel(len(proj) > 0, *refs),
        out_shape=out,
        in_specs=[pl.BlockSpec(memory_space=pltpu.SMEM), vm] + [hbm] * (8 + len(proj)),
        out_specs=out_spec,
        scratch_shapes=scratch,
        compiler_params=pltpu.CompilerParams(vmem_limit_bytes=16 << 20),
        cost_estimate=pl.CostEstimate(flops=1, bytes_accessed=1, transcendentals=0),
        name="section",
    )(where, x, *own, *other, *proj)


def gain_kernel(w_ref, gain_ref, out_ref):
    for i in range(gain_ref.shape[0]):
        span = slice(i * 128, (i + 1) * 128)
        column = jnp.transpose(jnp.broadcast_to(gain_ref[i:i + 1, :], (128, 128)))
        out_ref[span, :] = (w_ref[span, :].astype(F32) * column).astype(BF)


def pack_kernel(a_ref, o_ref, u_ref, d_ref, out_ref):
    width = o_ref.shape[1]
    for i in range(3):
        out_ref[i] = a_ref[:, i * width:(i + 1) * width]
    out_ref[3] = o_ref[...]
    for i in range(4):
        out_ref[4 + i] = u_ref[:, i * width:(i + 1) * width]
        out_ref[8 + i] = d_ref[8 * i:8 * i + 8]


def after_kernel(*refs):
    pass


def after(first, arrays):
    hbm = pl.BlockSpec(memory_space=pl.ANY)
    return pl.pallas_call(
        after_kernel,
        out_shape=[jax.ShapeDtypeStruct(v.shape, v.dtype) for v in arrays],
        in_specs=[hbm] * (len(first) + len(arrays)),
        out_specs=[hbm] * len(arrays),
        input_output_aliases={i + len(first): i for i in range(len(arrays))},
        compiler_params=pltpu.CompilerParams(vmem_limit_bytes=1 << 20),
        cost_estimate=pl.CostEstimate(flops=1, bytes_accessed=1, transcendentals=0),
        name="after",
    )(*first, *arrays)


def body(bar_in, section_weight, section_gain, projection, char_ids, lengths, char_embed, char_pos,
         attn_in, attn_out, ffn_in, ffn_out, norm_gain):
    y, core = lax.axis_index("y"), lax.axis_index("c")
    chip = lax.axis_index("x") * 4 + lax.axis_index("z")
    width = char_embed.shape[1]

    def swap(v):
        return lax.ppermute(v, "c", [(0, 1), (1, 0)])

    def turn(v, by):
        return lax.ppermute(v, "y", [(i, (i + by) % 4) for i in range(4)])

    def ordered(mine, theirs, axis):
        return jnp.where(core == 0, jnp.concatenate([mine, theirs], axis), jnp.concatenate([theirs, mine], axis))

    def spread(v):
        return lax.all_to_all(v, ("x", "z"), 0, 0, tiled=True)

    pack = pl.pallas_call(
        pack_kernel, out_shape=jax.ShapeDtypeStruct((12, 8, width), BF), name="pack",
    )(attn_in, attn_out, ffn_in, ffn_out)
    pack = lax.all_gather(pack.reshape(96, width), GROUP, axis=0, tiled=True).reshape(128, 12, 8, width)

    feats = bar_in.shape[2]
    weight = pl.pallas_call(
        gain_kernel, out_shape=jax.ShapeDtypeStruct(section_weight.shape[1:], BF),
        compiler_params=pltpu.CompilerParams(vmem_limit_bytes=8 << 20), name="gain",
    )(section_weight[0], section_gain.reshape(-1, 128))

    by_core = lax.dynamic_index_in_dim(bar_in, y, 0, keepdims=False).reshape(16, 2, 4, feats)
    by_core = by_core.transpose(1, 0, 2, 3).reshape(2, 64, feats)
    mine = lax.dynamic_index_in_dim(by_core, core, 0, keepdims=False)
    theirs = swap(lax.dynamic_index_in_dim(by_core, 1 - core, 0, keepdims=False))
    block = ordered(mine, theirs, 1)

    out = jnp.broadcast_to(block[None], (16,) + block.shape)
    x = spread(out)
    own = [weight, *after([x], [turn(weight, by) for by in (1, 2, 3)])]
    other = [swap(w) for w in own]
    proj = [projection, swap(projection)]
    for step in range(4):
        if step:
            x = spread(out)
        where = jnp.stack([lax.rem(y - step + 4, 4), core, chip])
        out = section_step(where, x, own, other, proj if step == 3 else None)
    parts = spread(out)
    return char_decode(parts, char_ids[0], lengths[0], char_embed, char_pos, norm_gain, pack)[None]


def solution(mesh):
    fine = jax.sharding.Mesh(mesh.devices.reshape(4, 4, 4, 2), GROUP)
    bar = ("x", "z", "c")
    in_specs = (
        P(None, None, bar),
        P("y", None, bar),
        P("y", None),
        P(bar, None),
        P("y", bar, None),
        P("y", bar),
        P(),
        P(),
        P(GROUP, None),
        P(GROUP, None),
        P(GROUP, None),
        P(GROUP, None),
        P(),
    )
    return jax.shard_map(body, mesh=fine, in_specs=in_specs, out_specs=P("y", bar, None), check_vma=False)
```

```python
import functools
import jax, jax.numpy as jnp
from jax import lax
from jax.sharding import PartitionSpec as P
from jax.experimental import pallas as pl
from jax.experimental.pallas import tpu as pltpu

BF=jnp.bfloat16
F32=jnp.float32

def rms_rows(v, g):
    return v * lax.rsqrt(jnp.mean(v * v, axis=-1, keepdims=True) + 1e-05) * g


HEADS = 16
VMEM_BYTES = 63_000_000


def embedded(prev, embed_ref, pos_ref):
    one_hot = (lax.broadcasted_iota(jnp.int32, (embed_ref.shape[0], prev.shape[1]), 0) == prev).astype(BF)
    rows = lax.dot_general(one_hot, embed_ref[...], (((0,), (0,)), ((), ())), preferred_element_type=F32)
    return rows + pos_ref[...].astype(F32)


def fetched(sources, refs, sems):
    copies = [pltpu.make_async_copy(source, to, sems.at[i]) for i, (source, to) in enumerate(zip(sources, refs))]
    for copy in copies:
        copy.start()
    return copies


def early_kernel(gate_ref, prev_in, embed_in, pos_in, gain_in, pack_ref, q_out, acc_out, top_out, sum_out,
                 prev_ref, embed_ref, pos_ref, gain_ref, n_ref, k_ref, v_ref, wq, sems, small_sems):
    bars, chars = prev_ref.shape
    vocab, width = embed_ref.shape
    small = fetched((prev_in, embed_in, pos_in, gain_in), (prev_ref, embed_ref, pos_ref, gain_ref), small_sems)
    copies = [pltpu.make_async_copy(pack_ref.at[:, j], wq.at[j], sems.at[j]) for j in range(3)]
    for copy in small:
        copy.wait()
    copies[0].start()
    for b in range(bars):
        emb = embedded(prev_ref[b:b + 1, :], embed_ref, pos_ref)
        n_ref[b * chars:(b + 1) * chars] = rms_rows(emb, gain_ref[0:1]).astype(BF)
    for j, dst in ((0, q_out), (1, k_ref), (2, v_ref)):
        copies[j].wait()
        if j < 2:
            copies[j + 1].start()
        dst[...] = jnp.dot(n_ref[...], wq[j].reshape(width, width), preferred_element_type=F32).astype(BF)
    low = lax.broadcasted_iota(jnp.int32, (chars, 128), 1) < 64
    query = lax.broadcasted_iota(jnp.int32, (chars, chars), 0)
    key = lax.broadcasted_iota(jnp.int32, (chars, chars), 1)
    seen = (query >= key) & (key > 0)
    head = lax.broadcasted_iota(jnp.int32, (chars, HEADS), 1)

    def attend(b, carry):
        rows = pl.ds(pl.multiple_of(b * chars, chars), chars)
        tops = jnp.full((chars, HEADS), -1e30, F32)
        sums = jnp.zeros((chars, HEADS), F32)
        for h in range(width // 128):
            cols = slice(h * 128, (h + 1) * 128)
            q, k, v = q_out[rows, cols], k_ref[rows, cols], v_ref[rows, cols]
            zero = jnp.zeros_like(k)
            kk = jnp.concatenate([jnp.where(low, k, zero), jnp.where(low, zero, k)], axis=0)
            vv = jnp.concatenate([jnp.where(low, v, zero), jnp.where(low, zero, v)], axis=0)
            s = lax.dot_general(q, kk, (((1,), (1,)), ((), ())), preferred_element_type=F32)
            probs = []
            for half in range(2):
                t = jnp.where(seen, s[:, half * chars:(half + 1) * chars], -1e30)
                top = jnp.max(t, axis=-1, keepdims=True)
                e = jnp.where(seen, jnp.exp((t - top) * 0.125), 0.0)
                tops = jnp.where(head == 2 * h + half, top, tops)
                sums = jnp.where(head == 2 * h + half, jnp.sum(e, axis=-1, keepdims=True), sums)
                probs.append(e.astype(BF))
            acc_out[rows, cols] = jnp.dot(jnp.concatenate(probs, axis=1), vv, preferred_element_type=F32)
        top_out[rows] = tops
        sum_out[rows] = sums
        return carry

    lax.fori_loop(0, bars, attend, 0)


def early_decode(gate, prev, embed, pos, gain, pack):
    bars, chars = prev.shape
    width = embed.shape[1]
    tokens = bars * chars
    t = lambda d, w=width: jax.ShapeDtypeStruct((tokens, w), d)
    return pl.pallas_call(
        early_kernel,
        out_shape=[t(BF), t(F32), t(F32, HEADS), t(F32, HEADS)],
        in_specs=[pl.BlockSpec(memory_space=pl.ANY)] * 6,
        out_specs=[pl.BlockSpec(memory_space=pltpu.VMEM)] * 4,
        scratch_shapes=[pltpu.VMEM(v.shape, v.dtype) for v in (prev, embed, pos, gain)]
        + [pltpu.VMEM((tokens, width), BF)] * 3
        + [pltpu.VMEM((3, 128, 8, width), BF), pltpu.SemaphoreType.DMA((3,)), pltpu.SemaphoreType.DMA((4,))],
        compiler_params=pltpu.CompilerParams(vmem_limit_bytes=VMEM_BYTES),
        cost_estimate=pl.CostEstimate(flops=8 << 30, bytes_accessed=16 << 20, transcendentals=1 << 20),
        name="early",
    )(gate, prev, embed, pos, gain, pack)


def late_kernel(*refs):
    pack_ref, out_ref, refs, sources = refs[11], refs[12], refs[13:], refs[:11]
    held, (x_ref, n_ref, c_ref, mid_ref, wk, wo, wup, wdn, sems, loads) = refs[:11], refs[11:]
    parts_ref, ids_ref, prev_ref, len_ref, embed_ref, pos_ref, gain_ref, top_in, sum_in, q_ref, acc_ref = held
    bars, chars = ids_ref.shape
    vocab, width = embed_ref.shape
    copies = [pltpu.make_async_copy(pack_ref.at[:, 1 + j], wk.at[j], sems.at[j]) for j in range(2)]
    copies.append(pltpu.make_async_copy(pack_ref.at[:, 3], wo, sems.at[2]))
    for j in range(4):
        copies.append(pltpu.make_async_copy(pack_ref.at[:, 4 + j], wup.at[j], sems.at[3 + j]))
    for j in range(4):
        rows = pl.ds(32 * j, 32)
        copies.append(pltpu.make_async_copy(pack_ref.at[rows, 8:12], wdn.at[rows], sems.at[7 + j]))
    small = [pltpu.make_async_copy(source, to, loads.at[i]) for i, (source, to) in enumerate(zip(sources, held))]
    for copy in small[:7] + copies[:2]:
        copy.start()
    for copy in small[:7]:
        copy.wait()
    for b in range(bars):
        x_ref[b * chars:(b + 1) * chars] = embedded(prev_ref[b:b + 1, :], embed_ref, pos_ref)
    vec = jnp.sum(parts_ref[...], axis=0).astype(BF).astype(F32)
    first = vec + pos_ref[0:1].astype(F32)
    normed = rms_rows(first, gain_ref[0:1]).astype(BF)
    kv = []
    for j in range(2):
        copies[j].wait()
        if j == 0:
            for copy in small[7:]:
                copy.start()
        kv.append(jnp.dot(normed, wk[j].reshape(width, width), preferred_element_type=F32).astype(BF).astype(F32))
    member = (lax.broadcasted_iota(jnp.int32, (HEADS, width), 1) // 64
              == lax.broadcasted_iota(jnp.int32, (HEADS, width), 0))
    expand = member.astype(BF)

    for copy in small[7:]:
        copy.wait()
    copies[2].start()
    copies[3].start()

    def widen(v):
        high = v.astype(BF)
        rest = (v - high.astype(F32)).astype(BF)
        both = jnp.concatenate([high, rest], axis=1)
        return jnp.dot(both, jnp.concatenate([expand, expand], axis=0), preferred_element_type=F32)

    for b in range(bars):
        rows = slice(b * chars, (b + 1) * chars)
        key = jnp.where(member, kv[0][b:b + 1], 0.0).astype(BF)
        score = lax.dot_general(q_ref[rows, :], key, (((1,), (1,)), ((), ())), preferred_element_type=F32)
        start = lax.broadcasted_iota(jnp.int32, (chars, HEADS), 0) == 0
        before = jnp.where(start, -1e30, top_in[rows, :])
        score = jnp.where(start, 0.0, score)
        top = jnp.maximum(before, score)
        old = jnp.exp((before - top) * 0.125)
        new = jnp.exp((score - top) * 0.125)
        inverse = 1.0 / (old * sum_in[rows, :] + new)
        mixed = acc_ref[rows, :] * widen(old * inverse) + kv[1][b:b + 1] * widen(new * inverse)
        c_ref[rows, :] = mixed.astype(BF)
        x_ref[b * chars:b * chars + 1, :] = first[b:b + 1]
    copies[2].wait()
    copies[7].start()
    copies[4].start()
    hidden = x_ref[...] + jnp.dot(c_ref[...], wo[...].reshape(width, width), preferred_element_type=F32)
    x_ref[...] = hidden
    n_ref[...] = rms_rows(hidden, gain_ref[1:2]).astype(BF)
    for j in range(4):
        copies[3 + j].wait()
        if j < 3:
            copies[8 + j].start()
        if j < 2:
            copies[5 + j].start()
        mid_ref[...] = jax.nn.gelu(jnp.dot(n_ref[...], wup[j].reshape(width, width), preferred_element_type=F32)).astype(BF)
        copies[7 + j].wait()
        x_ref[...] += jnp.dot(mid_ref[...], wdn[32 * j:32 * j + 32].reshape(width, width), preferred_element_type=F32)
    last = rms_rows(x_ref[...], gain_ref[2:3]).astype(BF)
    logits = lax.dot_general(embed_ref[...], last, (((1,), (1,)), ((), ())), preferred_element_type=F32)
    top = jnp.max(logits, axis=0, keepdims=True)
    norm = top + jnp.log(jnp.sum(jnp.exp(logits - top), axis=0, keepdims=True))
    for b in range(bars):
        cols = slice(b * chars, (b + 1) * chars)
        hit = lax.broadcasted_iota(jnp.int32, (vocab, chars), 0) == ids_ref[b:b + 1, :]
        picked = jnp.sum(jnp.where(hit, logits[:, cols], 0.0), axis=0, keepdims=True) - norm[:, cols]
        live = lax.broadcasted_iota(jnp.int32, (1, chars), 1) < len_ref[b:b + 1, :]
        out_ref[b:b + 1, :] = jnp.where(live, picked, 0.0)


def late_decode(parts, early, ids, prev, lengths, embed, pos, gain, pack):
    bars, chars = ids.shape
    width = embed.shape[1]
    tokens = bars * chars
    sources = (parts, ids, prev, lengths, embed, pos, gain, early[2], early[3], early[0], early[1])
    t = lambda d: pltpu.VMEM((tokens, width), d)
    return pl.pallas_call(
        late_kernel,
        out_shape=jax.ShapeDtypeStruct((bars, chars), F32),
        in_specs=[pl.BlockSpec(memory_space=pl.ANY)] * 12,
        out_specs=pl.BlockSpec(memory_space=pltpu.VMEM),
        scratch_shapes=[pltpu.VMEM(v.shape, v.dtype) for v in sources] + [t(F32), t(BF), t(BF), t(BF),
                        pltpu.VMEM((2, 128, 8, width), BF), pltpu.VMEM((128, 8, width), BF),
                        pltpu.VMEM((4, 128, 8, width), BF), pltpu.VMEM((128, 4, 8, width), BF),
                        pltpu.SemaphoreType.DMA((11,)), pltpu.SemaphoreType.DMA((11,))],
        compiler_params=pltpu.CompilerParams(vmem_limit_bytes=VMEM_BYTES),
        cost_estimate=pl.CostEstimate(flops=10 << 30, bytes_accessed=24 << 20, transcendentals=4 << 20),
        name="late",
    )(*sources, pack)


def shifted(ids):
    return jnp.concatenate([jnp.full((ids.shape[0], 1), -1, jnp.int32), ids[:, :-1]], axis=1)


GROUP = ("y", "x", "z", "c")


def section_kernel(step, project, x_in, *refs):
    own, other, refs = refs[:8], refs[8:16], refs[16:]
    if project:
        proj_own, proj_other, _, out_ref, x_ref, w_ref, sems, p_ref, p_sems = refs
    else:
        out_ref, x_ref, w_ref, sems, row_ref, out_sems = refs
    blocks, rows, cols = x_ref.shape
    side, depth = cols // 2, blocks * cols
    half = depth // 2
    core = lax.axis_index("c")
    which = lax.rem(lax.axis_index("y") - step + 4, 4)
    chip = lax.axis_index("x") * 4 + lax.axis_index("z")
    load_x = pltpu.make_async_copy(x_in, x_ref, sems.at[4])
    load_x.start()
    for i in range(4):
        @pl.when(which == i)
        def _():
            for part in range(2):
                for sources, at, sem in ((own, core, 0), (other, 1 - core, 1)):
                    lanes = pl.ds(pl.multiple_of(at * side, side), side)
                    pltpu.make_async_copy(
                        sources[2 * i + part], w_ref.at[pl.ds(part * half, half), lanes], sems.at[2 * part + sem]
                    ).start()
    if project:
        deep = proj_own.shape[0]
        loads = [
            pltpu.make_async_copy(source, p_ref.at[pl.ds(pl.multiple_of(at * deep, deep), deep)], p_sems.at[i])
            for i, (source, at) in enumerate(((proj_own, core), (proj_other, 1 - core)))
        ]
        for load in loads:
            load.start()
    load_x.wait()
    total = jnp.zeros((rows, cols), F32)
    for j in range(blocks):
        v = x_ref[j].astype(F32)
        total += v * v
    scale = lax.rsqrt(jnp.sum(total, axis=-1, keepdims=True) / depth + 1e-05)
    update = jnp.zeros((rows, cols), F32)
    for part in range(2):
        span = pl.ds(part * half, half)
        for sem in range(2):
            at = w_ref.at[span, pl.ds(sem * side, side)]
            pltpu.make_async_copy(own[0], at, sems.at[2 * part + sem]).wait()
        wide = jnp.concatenate([x_ref[part * blocks // 2 + j] for j in range(blocks // 2)], axis=1)
        update += jnp.dot(wide, w_ref[span, :], preferred_element_type=F32)
    leaving = (x_ref[chip].astype(F32) + jax.nn.gelu(update * scale)).astype(BF)
    if project:
        for load in loads:
            load.wait()
        partial = jnp.dot(leaving, p_ref[...], preferred_element_type=F32)
        each = rows // blocks
        for j in range(blocks):
            out_ref[j] = partial[j * each:(j + 1) * each]
    else:
        row_ref[...] = leaving
        sends = [pltpu.make_async_copy(row_ref, out_ref.at[j], out_sems.at[j]) for j in range(blocks)]
        for send in sends:
            send.start()
        for send in sends:
            send.wait()


def section_step(step, x, own, other, proj=()):
    blocks, rows, cols = x.shape
    vm = pl.BlockSpec(memory_space=pltpu.VMEM)
    hbm = pl.BlockSpec(memory_space=pl.ANY)
    scratch = [pltpu.VMEM(x.shape, BF), pltpu.VMEM((blocks * cols, cols), BF), pltpu.SemaphoreType.DMA((5,))]
    if not proj:
        out = jax.ShapeDtypeStruct(x.shape, BF)
        scratch += [pltpu.VMEM((rows, cols), BF), pltpu.SemaphoreType.DMA((blocks,))]
    else:
        width = proj[0].shape[1]
        out = jax.ShapeDtypeStruct((blocks, rows // blocks, width), F32)
        scratch += [pltpu.VMEM((cols, width), BF), pltpu.SemaphoreType.DMA((2,))]
    return pl.pallas_call(
        lambda *refs: section_kernel(step, len(proj) > 0, *refs),
        out_shape=out,
        in_specs=[hbm] * (17 + len(proj)),
        out_specs=vm if proj else hbm,
        scratch_shapes=scratch,
        compiler_params=pltpu.CompilerParams(vmem_limit_bytes=VMEM_BYTES),
        cost_estimate=pl.CostEstimate(flops=1, bytes_accessed=1, transcendentals=0),
        name="section",
    )(x, *own, *other, *proj)


def prepare_kernel(*refs):
    sources, outs, scratch = refs[:6], refs[6:9], refs[9:]
    held, (pack_ref, sems, out_sem) = scratch[:6], scratch[6:]
    loads = [pltpu.make_async_copy(source, to, sems.at[i]) for i, (source, to) in enumerate(zip(sources, held))]
    for load in loads:
        load.start()
    a_ref, o_ref, u_ref, d_ref, w_ref, gain_ref = held
    width = o_ref.shape[1]
    for load in loads[:4]:
        load.wait()
    for i in range(3):
        pack_ref[i] = a_ref[:, i * width:(i + 1) * width]
    pack_ref[3] = o_ref[...]
    for i in range(4):
        pack_ref[4 + i] = u_ref[:, i * width:(i + 1) * width]
        pack_ref[8 + i] = d_ref[8 * i:8 * i + 8]
    store = pltpu.make_async_copy(pack_ref, outs[0], out_sem)
    store.start()
    loads[4].wait()
    loads[5].wait()
    rows = outs[1].shape[0]
    for i in range(gain_ref.shape[0]):
        span = slice(i * 128, (i + 1) * 128)
        column = jnp.transpose(jnp.broadcast_to(gain_ref[i:i + 1, :], (128, 128)))
        first = i * 128 % rows
        outs[1 + i * 128 // rows][first:first + 128] = (w_ref[span, :].astype(F32) * column).astype(BF)
    store.wait()


def prepare(*sources):
    depth, cols = sources[4].shape
    width = sources[1].shape[1]
    hbm = pl.BlockSpec(memory_space=pl.ANY)
    vm = pl.BlockSpec(memory_space=pltpu.VMEM)
    half = jax.ShapeDtypeStruct((depth // 2, cols), BF)
    return pl.pallas_call(
        prepare_kernel,
        out_shape=[jax.ShapeDtypeStruct((12, 8, width), BF), half, half],
        in_specs=[hbm] * 6,
        out_specs=[hbm, vm, vm],
        scratch_shapes=[pltpu.VMEM(v.shape, v.dtype) for v in sources]
        + [pltpu.VMEM((12, 8, width), BF), pltpu.SemaphoreType.DMA((6,)), pltpu.SemaphoreType.DMA],
        compiler_params=pltpu.CompilerParams(vmem_limit_bytes=VMEM_BYTES),
        name="prepare",
    )(*sources)


def after_kernel(*refs):
    pass


def after(first, arrays):
    hbm = pl.BlockSpec(memory_space=pl.ANY)
    return pl.pallas_call(
        after_kernel,
        out_shape=[jax.ShapeDtypeStruct(v.shape, v.dtype) for v in arrays],
        in_specs=[hbm] * (len(first) + len(arrays)),
        out_specs=[hbm] * len(arrays),
        input_output_aliases={i + len(first): i for i in range(len(arrays))},
        compiler_params=pltpu.CompilerParams(vmem_limit_bytes=1 << 20),
        cost_estimate=pl.CostEstimate(flops=1, bytes_accessed=1, transcendentals=0),
        name="after",
    )(*first, *arrays)


def body(bar_in, section_weight, section_gain, projection, char_ids, lengths, char_embed, char_pos,
         attn_in, attn_out, ffn_in, ffn_out, norm_gain):
    y, core = lax.axis_index("y"), lax.axis_index("c")
    width = char_embed.shape[1]

    def swap(v):
        return lax.ppermute(v, "c", [(0, 1), (1, 0)])

    def turn(v, by):
        return lax.ppermute(v, "y", [(i, (i + by) % 4) for i in range(4)])

    def ordered(mine, theirs, axis):
        return jnp.where(core == 0, jnp.concatenate([mine, theirs], axis), jnp.concatenate([theirs, mine], axis))

    feats = bar_in.shape[2]
    pack, low, high = prepare(
        attn_in, attn_out, ffn_in, ffn_out, section_weight[0], section_gain.reshape(-1, 128))
    pack = lax.all_gather(pack.reshape(96, width), GROUP, axis=0, tiled=True).reshape(128, 12, 8, width)

    by_core = lax.dynamic_index_in_dim(bar_in, y, 0, keepdims=False).reshape(16, 2, 4, feats)
    by_core = by_core.transpose(1, 0, 2, 3).reshape(2, 64, feats)
    mine = lax.dynamic_index_in_dim(by_core, core, 0, keepdims=False)
    theirs = swap(lax.dynamic_index_in_dim(by_core, 1 - core, 0, keepdims=False))
    block = ordered(mine, theirs, 1)

    def spread(v):
        return lax.all_to_all(v, ("x", "z"), 0, 0, tiled=True)

    x = spread(jnp.broadcast_to(block[None], (16,) + block.shape))
    below_low, above_high, below_high, above_low = after(
        [x], [turn(low, 1), turn(high, 3), turn(high, 1), turn(low, 3)])
    own = [low, high, below_low, below_high, turn(below_low, 1), turn(above_high, 3), above_low, above_high]
    other = [swap(w) for w in own]
    proj = [projection, swap(projection)]
    for step in range(4):
        if step:
            x = spread(out)
        out = section_step(step, x, own, other, [*proj, early[2]] if step == 3 else ())
        if step == 2:
            ids, prev = char_ids[0], shifted(char_ids[0])
            early = early_decode(out, prev, char_embed, char_pos, norm_gain, pack)
    parts = spread(out)
    return late_decode(parts, early, ids, prev, lengths[0][:, None], char_embed, char_pos, norm_gain, pack)[None]


def solution(mesh):
    fine = jax.sharding.Mesh(mesh.devices.reshape(4, 4, 4, 2), GROUP)
    bar = ("x", "z", "c")
    in_specs = (
        P(None, None, bar),
        P("y", None, bar),
        P("y", None),
        P(bar, None),
        P("y", bar, None),
        P("y", bar),
        P(),
        P(),
        P(GROUP, None),
        P(GROUP, None),
        P(GROUP, None),
        P(GROUP, None),
        P(),
    )
    return jax.shard_map(body, mesh=fine, in_specs=in_specs, out_specs=P("y", bar, None), check_vma=False)
```

```python
import functools
import jax, jax.numpy as jnp
from jax import lax
from jax.sharding import PartitionSpec as P
from jax.experimental import pallas as pl
from jax.experimental.pallas import tpu as pltpu

BF=jnp.bfloat16
F32=jnp.float32

def rms_rows(v, g):
    return v * lax.rsqrt(jnp.mean(v * v, axis=-1, keepdims=True) + 1e-05) * g


HEADS = 16
VMEM_BYTES = 63_000_000


def embedded(prev, embed_ref, pos_ref):
    one_hot = (lax.broadcasted_iota(jnp.int32, (embed_ref.shape[0], prev.shape[1]), 0) == prev).astype(BF)
    rows = lax.dot_general(one_hot, embed_ref[...], (((0,), (0,)), ((), ())), preferred_element_type=F32)
    return rows + pos_ref[...].astype(F32)


def fetched(sources, refs, sems):
    copies = [pltpu.make_async_copy(source, to, sems.at[i]) for i, (source, to) in enumerate(zip(sources, refs))]
    for copy in copies:
        copy.start()
    return copies


def embed_kernel(prev_ref, embed_ref, pos_ref, gain_ref, out_ref):
    bars, chars = prev_ref.shape
    for b in range(bars):
        emb = embedded(prev_ref[b:b + 1, :], embed_ref, pos_ref)
        out_ref[b * chars:(b + 1) * chars] = rms_rows(emb, gain_ref[0:1]).astype(BF)


def embed_chars(prev, embed, pos, gain):
    vm = pl.BlockSpec(memory_space=pltpu.VMEM)
    return pl.pallas_call(
        embed_kernel,
        out_shape=jax.ShapeDtypeStruct((prev.size, embed.shape[1]), BF),
        in_specs=[vm] * 4,
        out_specs=vm,
        compiler_params=pltpu.CompilerParams(vmem_limit_bytes=VMEM_BYTES),
        name="embed",
    )(prev, embed, pos, gain)


def early_kernel(gate_ref, n_in, pack_ref, q_out, acc_out, top_out, sum_out,
                 q_ref, acc_ref, top_ref, sum_ref, n_ref, k_ref, v_ref, wq, sems, out_sems):
    tokens, width = n_ref.shape
    chars = 128
    bars = tokens // chars
    copies = [pltpu.make_async_copy(pack_ref.at[:, j], wq.at[j], sems.at[j]) for j in range(3)]
    load = pltpu.make_async_copy(n_in, n_ref, sems.at[3])
    load.start()
    copies[0].start()
    load.wait()
    q_store = pltpu.make_async_copy(q_ref, q_out, out_sems.at[3 * bars])
    for j, dst in ((0, q_ref), (1, k_ref), (2, v_ref)):
        copies[j].wait()
        if j < 2:
            copies[j + 1].start()
        made = jnp.dot(n_ref[...], wq[j].reshape(width, width), preferred_element_type=F32).astype(BF)
        dst[...] = made * BF(0.125) if j == 0 else made
        if j == 0:
            q_store.start()

    def stores(b):
        rows = pl.ds(pl.multiple_of(b * chars, chars), chars)
        return [pltpu.make_async_copy(source.at[rows], to.at[rows], out_sems.at[3 * b + i])
                for i, (source, to) in enumerate(((acc_ref, acc_out), (top_ref, top_out), (sum_ref, sum_out)))]

    low = lax.broadcasted_iota(jnp.int32, (chars, 128), 1) < 64
    query = lax.broadcasted_iota(jnp.int32, (chars, chars), 0)
    key = lax.broadcasted_iota(jnp.int32, (chars, chars), 1)
    seen = (query >= key) & (key > 0)
    second = lax.broadcasted_iota(jnp.int32, (2 * chars, 128), 0) // chars
    column = lax.broadcasted_iota(jnp.int32, (2 * chars, 128), 1)

    def attend(b, carry):
        rows = pl.ds(pl.multiple_of(b * chars, chars), chars)
        tops = jnp.full((chars, 128), -1e30, F32)
        sums = jnp.zeros((chars, 128), F32)
        for h in range(width // 128):
            cols = slice(h * 128, (h + 1) * 128)
            q, k, v = q_ref[rows, cols], k_ref[rows, cols], v_ref[rows, cols]
            zero = jnp.zeros_like(k)
            kk = jnp.concatenate([jnp.where(low, k, zero), jnp.where(low, zero, k)], axis=0)
            vv = jnp.concatenate([jnp.where(low, v, zero), jnp.where(low, zero, v)], axis=0)
            ones = (column == 2 * h + second).astype(F32).astype(BF)
            s = lax.dot_general(q, kk, (((1,), (1,)), ((), ())), preferred_element_type=F32)
            probs = []
            for half in range(2):
                t = jnp.where(seen, s[:, half * chars:(half + 1) * chars], -1e30)
                top = jnp.max(t, axis=-1, keepdims=True)
                tops = jnp.where(key == 2 * h + half, top, tops)
                probs.append(jnp.exp(t - top).astype(BF))
            both = jnp.dot(jnp.concatenate(probs, axis=1), jnp.concatenate([vv, ones], axis=1), preferred_element_type=F32)
            acc_ref[rows, cols] = both[:, :128]
            sums += both[:, 128:]
        top_ref[rows] = tops
        sum_ref[rows] = sums
        for store in stores(b):
            store.start()
        return carry

    lax.fori_loop(0, bars, attend, 0)
    q_store.wait()
    for b in range(bars):
        for store in stores(b):
            store.wait()


def early_decode(gate, normed, pack):
    tokens, width = normed.shape
    hbm = pl.BlockSpec(memory_space=pl.ANY)
    shapes = ((width, BF), (width, F32), (128, F32), (128, F32))
    return pl.pallas_call(
        early_kernel,
        out_shape=[jax.ShapeDtypeStruct((tokens, w), d) for w, d in shapes],
        in_specs=[hbm] * 3,
        out_specs=[hbm] * 4,
        scratch_shapes=[pltpu.VMEM((tokens, w), d) for w, d in shapes]
        + [pltpu.VMEM((tokens, width), BF)] * 3
        + [pltpu.VMEM((3, 128, 8, width), BF), pltpu.SemaphoreType.DMA((4,)), pltpu.SemaphoreType.DMA((13,))],
        compiler_params=pltpu.CompilerParams(vmem_limit_bytes=VMEM_BYTES),
        cost_estimate=pl.CostEstimate(flops=8 << 30, bytes_accessed=16 << 20, transcendentals=1 << 20),
        name="early",
    )(gate, normed, pack)


def late_kernel(*refs):
    pack_ref, out_ref, refs, sources = refs[11], refs[12], refs[13:], refs[:11]
    held, (x_ref, n_ref, c_ref, mid_ref, wk, wo, wup, wdn, sems, loads) = refs[:11], refs[11:]
    parts_ref, ids_ref, prev_ref, len_ref, embed_ref, pos_ref, gain_ref, top_in, sum_in, q_ref, acc_ref = held
    bars, chars = ids_ref.shape
    vocab, width = embed_ref.shape
    copies = [pltpu.make_async_copy(pack_ref.at[:, 1 + j], wk.at[j], sems.at[j]) for j in range(2)]
    copies.append(pltpu.make_async_copy(pack_ref.at[:, 3], wo, sems.at[2]))
    for j in range(4):
        copies.append(pltpu.make_async_copy(pack_ref.at[:, 4 + j], wup.at[j], sems.at[3 + j]))
    for j in range(4):
        rows = pl.ds(32 * j, 32)
        copies.append(pltpu.make_async_copy(pack_ref.at[rows, 8:12], wdn.at[rows], sems.at[7 + j]))
    small = [pltpu.make_async_copy(source, to, loads.at[i]) for i, (source, to) in enumerate(zip(sources, held))]
    for copy in small[:7] + copies[:2]:
        copy.start()
    for copy in small[:7]:
        copy.wait()
    for copy in small[7:]:
        copy.start()
    for b in range(bars):
        x_ref[b * chars:(b + 1) * chars] = embedded(prev_ref[b:b + 1, :], embed_ref, pos_ref)
    vec = jnp.sum(parts_ref[...], axis=0).astype(BF).astype(F32)
    first = vec + pos_ref[0:1].astype(F32)
    normed = rms_rows(first, gain_ref[0:1]).astype(BF)
    kv = []
    for j in range(2):
        copies[j].wait()
        if j == 1:
            copies[2].start()
        kv.append(jnp.dot(normed, wk[j].reshape(width, width), preferred_element_type=F32).astype(BF).astype(F32))
    member = (lax.broadcasted_iota(jnp.int32, (HEADS, width), 1) // 64
              == lax.broadcasted_iota(jnp.int32, (HEADS, width), 0))
    expand = member.astype(BF)

    for copy in small[7:]:
        copy.wait()
    copies[3].start()
    copies[7].start()

    def widen(v):
        high = v.astype(BF)
        rest = (v - high.astype(F32)).astype(BF)
        both = jnp.concatenate([high, rest], axis=1)
        return jnp.dot(both, jnp.concatenate([expand, expand], axis=0), preferred_element_type=F32)

    for b in range(bars):
        rows = slice(b * chars, (b + 1) * chars)
        key = jnp.where(member, kv[0][b:b + 1], 0.0).astype(BF)
        score = lax.dot_general(q_ref[rows, :], key, (((1,), (1,)), ((), ())), preferred_element_type=F32)
        start = lax.broadcasted_iota(jnp.int32, (chars, HEADS), 0) == 0
        before = jnp.where(start, -1e30, top_in[rows, :HEADS])
        score = jnp.where(start, 0.0, score)
        top = jnp.maximum(before, score)
        old = jnp.exp(before - top)
        new = jnp.exp(score - top)
        inverse = 1.0 / (old * sum_in[rows, :HEADS] + new)
        mixed = acc_ref[rows, :] * widen(old * inverse) + kv[1][b:b + 1] * widen(new * inverse)
        c_ref[rows, :] = mixed.astype(BF)
        x_ref[b * chars:b * chars + 1, :] = first[b:b + 1]
    copies[2].wait()
    copies[4].start()
    hidden = x_ref[...] + jnp.dot(c_ref[...], wo[...].reshape(width, width), preferred_element_type=F32)
    x_ref[...] = hidden
    n_ref[...] = rms_rows(hidden, gain_ref[1:2]).astype(BF)
    for j in range(4):
        copies[3 + j].wait()
        if j < 3:
            copies[8 + j].start()
        if j < 2:
            copies[5 + j].start()
        mid_ref[...] = jax.nn.gelu(jnp.dot(n_ref[...], wup[j].reshape(width, width), preferred_element_type=F32)).astype(BF)
        copies[7 + j].wait()
        x_ref[...] += jnp.dot(mid_ref[...], wdn[32 * j:32 * j + 32].reshape(width, width), preferred_element_type=F32)
    last = rms_rows(x_ref[...], gain_ref[2:3]).astype(BF)
    logits = lax.dot_general(embed_ref[...], last, (((1,), (1,)), ((), ())), preferred_element_type=F32)
    top = jnp.max(logits, axis=0, keepdims=True)
    norm = top + jnp.log(jnp.sum(jnp.exp(logits - top), axis=0, keepdims=True))
    for b in range(bars):
        cols = slice(b * chars, (b + 1) * chars)
        hit = lax.broadcasted_iota(jnp.int32, (vocab, chars), 0) == ids_ref[b:b + 1, :]
        picked = jnp.sum(jnp.where(hit, logits[:, cols], 0.0), axis=0, keepdims=True) - norm[:, cols]
        live = lax.broadcasted_iota(jnp.int32, (1, chars), 1) < len_ref[b:b + 1, :]
        out_ref[b:b + 1, :] = jnp.where(live, picked, 0.0)


def late_decode(parts, early, ids, prev, lengths, embed, pos, gain, pack):
    bars, chars = ids.shape
    width = embed.shape[1]
    tokens = bars * chars
    sources = (parts, ids, prev, lengths, embed, pos, gain, early[2], early[3], early[0], early[1])
    t = lambda d: pltpu.VMEM((tokens, width), d)
    return pl.pallas_call(
        late_kernel,
        out_shape=jax.ShapeDtypeStruct((bars, chars), F32),
        in_specs=[pl.BlockSpec(memory_space=pl.ANY)] * 12,
        out_specs=pl.BlockSpec(memory_space=pltpu.VMEM),
        scratch_shapes=[pltpu.VMEM(v.shape, v.dtype) for v in sources] + [t(F32), t(BF), t(BF), t(BF),
                        pltpu.VMEM((2, 128, 8, width), BF), pltpu.VMEM((128, 8, width), BF),
                        pltpu.VMEM((4, 128, 8, width), BF), pltpu.VMEM((128, 4, 8, width), BF),
                        pltpu.SemaphoreType.DMA((11,)), pltpu.SemaphoreType.DMA((11,))],
        compiler_params=pltpu.CompilerParams(vmem_limit_bytes=VMEM_BYTES),
        cost_estimate=pl.CostEstimate(flops=10 << 30, bytes_accessed=24 << 20, transcendentals=4 << 20),
        name="late",
    )(*sources, pack)


def shifted(ids):
    return jnp.concatenate([jnp.full((ids.shape[0], 1), -1, jnp.int32), ids[:, :-1]], axis=1)


GROUP = ("y", "x", "z", "c")


def section_kernel(step, project, x_in, *refs):
    kept = 8 if project else 6 if step == 0 else 5
    weights, refs = refs[:-kept], refs[-kept:]
    if project:
        proj_own, proj_other, out_ref, x_ref, w_ref, sems, p_ref, p_sems = refs
    elif step == 0:
        out_ref, row_ref, x_ref, w_ref, sems, _ = refs
    else:
        out_ref, x_ref, w_ref, sems, row_ref = refs
    blocks, rows, cols = x_ref.shape
    side, depth = cols // 2, blocks * cols
    half = depth // 2
    y, core = lax.axis_index("y"), lax.axis_index("c")
    which = jnp.where(y < 2, (y, 1 - y, 3 - y, 2 + y)[step], (y - 2, y, y - 2, 3 - y)[step])
    chip = lax.axis_index("x") * 4 + lax.axis_index("z")
    load_x = pltpu.make_async_copy(x_in, x_ref, sems.at[4])
    load_x.start()
    held = [(weights[i], weights[i + 1]) for i in range(0, min(len(weights), 6), 2)]
    held += [(weights[6:8], weights[8:])] if len(weights) > 6 else []
    for i, pair in enumerate(held):
        @pl.when(which == i)
        def _():
            for part in range(2):
                span = pl.ds(part * half, half)
                for sem, at in ((0, core), (1, 1 - core)):
                    lanes = pl.ds(pl.multiple_of(at * side, side), side)
                    source = pair[sem].at[span] if i < 3 else pair[sem][part]
                    pltpu.make_async_copy(source, w_ref.at[span, lanes], sems.at[2 * part + sem]).start()
    if project:
        deep = proj_own.shape[0]
        loads = [
            pltpu.make_async_copy(source, p_ref.at[pl.ds(pl.multiple_of(at * deep, deep), deep)], p_sems.at[i])
            for i, (source, at) in enumerate(((proj_own, core), (proj_other, 1 - core)))
        ]
        for load in loads:
            load.start()
    load_x.wait()
    total = jnp.zeros((rows, cols), F32)
    for j in range(blocks):
        v = x_ref[j].astype(F32)
        total += v * v
    scale = lax.rsqrt(jnp.sum(total, axis=-1, keepdims=True) / depth + 1e-05)
    update = jnp.zeros((rows, cols), F32)
    for part in range(2):
        span = pl.ds(part * half, half)
        for sem in range(2):
            at = w_ref.at[span, pl.ds(sem * side, side)]
            pltpu.make_async_copy(weights[0].at[span], at, sems.at[2 * part + sem]).wait()
        wide = jnp.concatenate([x_ref[part * blocks // 2 + j] for j in range(blocks // 2)], axis=1)
        update += jnp.dot(wide, w_ref[span, :], preferred_element_type=F32)
    leaving = (x_ref[chip].astype(F32) + jax.nn.gelu(update * scale)).astype(BF)
    if project:
        for load in loads:
            load.wait()
        partial = jnp.dot(leaving, p_ref[...], preferred_element_type=F32)
        each = rows // blocks
        for j in range(blocks):
            out_ref[j] = partial[j * each:(j + 1) * each]
    elif step == 0:
        out_ref[...] = leaving[:rows // 2]
        row_ref[...] = leaving[rows // 2:]
    else:
        row_ref[...] = leaving
        sends = [pltpu.make_async_copy(row_ref, out_ref.at[j], sems.at[5 + j]) for j in range(blocks)]
        for send in sends:
            send.start()
        for send in sends:
            send.wait()


def section_step(step, x, weights, proj=()):
    blocks, rows, cols = x.shape
    vm = pl.BlockSpec(memory_space=pltpu.VMEM)
    hbm = pl.BlockSpec(memory_space=pl.ANY)
    scratch = [pltpu.VMEM(x.shape, BF), pltpu.VMEM((blocks * cols, cols), BF), pltpu.SemaphoreType.DMA((5 + blocks,))]
    if not proj:
        out = [jax.ShapeDtypeStruct((rows // 2, cols), BF)] * 2 if step == 0 else jax.ShapeDtypeStruct(x.shape, BF)
        scratch += [pltpu.VMEM((rows, cols), BF)]
    else:
        width = proj[0].shape[1]
        out = jax.ShapeDtypeStruct((blocks, rows // blocks, width), F32)
        scratch += [pltpu.VMEM((cols, width), BF), pltpu.SemaphoreType.DMA((2,))]
    return pl.pallas_call(
        lambda *refs: section_kernel(step, len(proj) > 0, *refs),
        out_shape=out,
        in_specs=[hbm] * (1 + len(weights) + len(proj)),
        out_specs=[vm, vm] if step == 0 else vm if proj else hbm,
        scratch_shapes=scratch,
        compiler_params=pltpu.CompilerParams(vmem_limit_bytes=VMEM_BYTES),
        cost_estimate=pl.CostEstimate(flops=1, bytes_accessed=1, transcendentals=0),
        name="section",
    )(x, *weights, *proj)


def prepare_kernel(*refs):
    sources, outs, scratch = refs[:6], refs[6:8], refs[8:]
    held, (pack_ref, sems, out_sem) = scratch[:6], scratch[6:]
    loads = [pltpu.make_async_copy(source, to, sems.at[i]) for i, (source, to) in enumerate(zip(sources, held))]
    for load in loads:
        load.start()
    a_ref, o_ref, u_ref, d_ref, w_ref, gain_ref = held
    width = o_ref.shape[1]
    for load in loads[:4]:
        load.wait()
    for i in range(3):
        pack_ref[i] = a_ref[:, i * width:(i + 1) * width]
    pack_ref[3] = o_ref[...]
    for i in range(4):
        pack_ref[4 + i] = u_ref[:, i * width:(i + 1) * width]
        pack_ref[8 + i] = d_ref[8 * i:8 * i + 8]
    store = pltpu.make_async_copy(pack_ref, outs[0], out_sem)
    store.start()
    loads[4].wait()
    loads[5].wait()
    for i in range(gain_ref.shape[0]):
        span = slice(i * 128, (i + 1) * 128)
        column = jnp.transpose(jnp.broadcast_to(gain_ref[i:i + 1, :], (128, 128)))
        outs[1][span, :] = (w_ref[span, :].astype(F32) * column).astype(BF)
    store.wait()


def prepare(*sources):
    depth, cols = sources[4].shape
    width = sources[1].shape[1]
    hbm = pl.BlockSpec(memory_space=pl.ANY)
    vm = pl.BlockSpec(memory_space=pltpu.VMEM)
    return pl.pallas_call(
        prepare_kernel,
        out_shape=[jax.ShapeDtypeStruct((12, 8, width), BF), jax.ShapeDtypeStruct((depth, cols), BF)],
        in_specs=[hbm] * 6,
        out_specs=[hbm, vm],
        scratch_shapes=[pltpu.VMEM(v.shape, v.dtype) for v in sources]
        + [pltpu.VMEM((12, 8, width), BF), pltpu.SemaphoreType.DMA((6,)), pltpu.SemaphoreType.DMA],
        compiler_params=pltpu.CompilerParams(vmem_limit_bytes=VMEM_BYTES),
        name="prepare",
    )(*sources)


def after_kernel(*refs):
    pass


def after(first, arrays):
    hbm = pl.BlockSpec(memory_space=pl.ANY)
    return pl.pallas_call(
        after_kernel,
        out_shape=[jax.ShapeDtypeStruct(v.shape, v.dtype) for v in arrays],
        in_specs=[hbm] * (len(first) + len(arrays)),
        out_specs=[hbm] * len(arrays),
        input_output_aliases={i + len(first): i for i in range(len(arrays))},
        compiler_params=pltpu.CompilerParams(vmem_limit_bytes=1 << 20),
        cost_estimate=pl.CostEstimate(flops=1, bytes_accessed=1, transcendentals=0),
        name="after",
    )(*first, *arrays)


def body(bar_in, section_weight, section_gain, projection, char_ids, lengths, char_embed, char_pos,
         attn_in, attn_out, ffn_in, ffn_out, norm_gain):
    y, core = lax.axis_index("y"), lax.axis_index("c")
    width = char_embed.shape[1]

    def swap(v):
        return lax.ppermute(v, "c", [(0, 1), (1, 0)])

    def across(v, *pairs):
        return lax.ppermute(v, "y", pairs)

    def ordered(mine, theirs, axis):
        return jnp.where(core == 0, jnp.concatenate([mine, theirs], axis), jnp.concatenate([theirs, mine], axis))

    feats = bar_in.shape[2]
    pack, weight = prepare(
        attn_in, attn_out, ffn_in, ffn_out, section_weight[0], section_gain.reshape(-1, 128))
    pack = lax.all_gather(pack.reshape(96, width), GROUP, axis=0, tiled=True).reshape(128, 12, 8, width)

    pair = jnp.stack([jnp.minimum(y, 3 - y), jnp.maximum(y, 3 - y)])
    by_core = jnp.concatenate([lax.dynamic_slice_in_dim(bar_in, pair[i], 1, 0) for i in range(2)])
    by_core = by_core.reshape(2, 16, 2, 4, feats).transpose(2, 0, 1, 3, 4).reshape(2, 128, feats)
    mine = lax.dynamic_index_in_dim(by_core, core, 0, keepdims=False)
    theirs = swap(lax.dynamic_index_in_dim(by_core, 1 - core, 0, keepdims=False))

    def spread(v):
        return lax.all_to_all(v, ("x", "z"), 0, 0, tiled=True)

    def copies(v):
        return jnp.broadcast_to(v[None], (16,) + v.shape)

    x = spread(copies(ordered(mine, theirs, 1)))
    near, far = after([x], [across(weight, (0, 1), (1, 0), (2, 3), (3, 2)), across(weight, (1, 2), (2, 1), (3, 0))])
    weights = [weight, swap(weight), near, swap(near)]
    half = near.shape[0] // 2
    farther = [across(far[:half], (0, 1), (1, 0), (2, 3)), across(near[half:], (0, 3), (3, 0), (2, 1))]
    far_other = swap(far)
    here, there = section_step(0, x, weights)
    there = across(after([far_other], [there])[0], (0, 3), (1, 2))
    x = spread(copies(jnp.where(y < 2, here, there)))
    farther = after([x], farther)
    weights += [far, far_other, *farther, *[swap(w) for w in farther]]
    normed = embed_chars(shifted(char_ids[0]), char_embed, char_pos, norm_gain)
    x = spread(section_step(1, x, weights))
    x = spread(section_step(2, x, weights))
    out = section_step(3, x, weights, [projection, swap(projection)])
    early = early_decode(out, normed, pack)
    parts = spread(out)
    return late_decode(parts, early, char_ids[0], shifted(char_ids[0]), lengths[0][:, None], char_embed, char_pos, norm_gain, pack)[None]


def solution(mesh):
    fine = jax.sharding.Mesh(mesh.devices.reshape(4, 4, 4, 2), GROUP)
    bar = ("x", "z", "c")
    in_specs = (
        P(None, None, bar),
        P("y", None, bar),
        P("y", None),
        P(bar, None),
        P("y", bar, None),
        P("y", bar),
        P(),
        P(),
        P(GROUP, None),
        P(GROUP, None),
        P(GROUP, None),
        P(GROUP, None),
        P(),
    )
    return jax.shard_map(body, mesh=fine, in_specs=in_specs, out_specs=P("y", bar, None), check_vma=False)
```

```python
import functools
import jax, jax.numpy as jnp
from jax import lax
from jax.sharding import PartitionSpec as P
from jax.experimental import pallas as pl
from jax.experimental.pallas import tpu as pltpu

BF=jnp.bfloat16
F32=jnp.float32

def rms_rows(v, g):
    return v * lax.rsqrt(jnp.mean(v * v, axis=-1, keepdims=True) + 1e-05) * g


HEADS = 16
VMEM_BYTES = 63_000_000


def embedded(prev, embed_ref, pos_ref):
    one_hot = (lax.broadcasted_iota(jnp.int32, (embed_ref.shape[0], prev.shape[1]), 0) == prev).astype(BF)
    rows = lax.dot_general(one_hot, embed_ref[...], (((0,), (0,)), ((), ())), preferred_element_type=F32)
    return rows + pos_ref[...].astype(F32)


def fetched(sources, refs, sems):
    copies = [pltpu.make_async_copy(source, to, sems.at[i]) for i, (source, to) in enumerate(zip(sources, refs))]
    for copy in copies:
        copy.start()
    return copies


def embed_kernel(prev_ref, embed_ref, pos_ref, gain_ref, out_ref):
    bars, chars = prev_ref.shape
    for b in range(bars):
        emb = embedded(prev_ref[b:b + 1, :], embed_ref, pos_ref)
        out_ref[b * chars:(b + 1) * chars] = rms_rows(emb, gain_ref[0:1]).astype(BF)


def embed_chars(prev, embed, pos, gain):
    vm = pl.BlockSpec(memory_space=pltpu.VMEM)
    return pl.pallas_call(
        embed_kernel,
        out_shape=jax.ShapeDtypeStruct((prev.size, embed.shape[1]), BF),
        in_specs=[vm] * 4,
        out_specs=vm,
        compiler_params=pltpu.CompilerParams(vmem_limit_bytes=VMEM_BYTES),
        name="embed",
    )(prev, embed, pos, gain)


def early_kernel(gate_ref, n_in, pack_ref, q_out, acc_out, top_out, sum_out,
                 q_ref, acc_ref, top_ref, sum_ref, n_ref, k_ref, v_ref, wq, sems, out_sems):
    tokens, width = n_ref.shape
    chars = 128
    bars = tokens // chars
    copies = [pltpu.make_async_copy(pack_ref.at[:, j], wq.at[j], sems.at[j]) for j in range(3)]
    load = pltpu.make_async_copy(n_in, n_ref, sems.at[3])
    load.start()
    copies[0].start()
    load.wait()
    q_store = pltpu.make_async_copy(q_ref, q_out, out_sems.at[3 * bars])
    for j, dst in ((0, q_ref), (1, k_ref), (2, v_ref)):
        copies[j].wait()
        if j < 2:
            copies[j + 1].start()
        made = jnp.dot(n_ref[...], wq[j].reshape(width, width), preferred_element_type=F32).astype(BF)
        dst[...] = made * BF(0.125) if j == 0 else made
        if j == 0:
            q_store.start()

    def stores(b):
        rows = pl.ds(pl.multiple_of(b * chars, chars), chars)
        return [pltpu.make_async_copy(source.at[rows], to.at[rows], out_sems.at[3 * b + i])
                for i, (source, to) in enumerate(((acc_ref, acc_out), (top_ref, top_out), (sum_ref, sum_out)))]

    low = lax.broadcasted_iota(jnp.int32, (chars, 128), 1) < 64
    query = lax.broadcasted_iota(jnp.int32, (chars, chars), 0)
    key = lax.broadcasted_iota(jnp.int32, (chars, chars), 1)
    seen = (query >= key) & (key > 0)
    second = lax.broadcasted_iota(jnp.int32, (2 * chars, 128), 0) // chars
    column = lax.broadcasted_iota(jnp.int32, (2 * chars, 128), 1)

    def attend(b, carry):
        rows = pl.ds(pl.multiple_of(b * chars, chars), chars)
        tops = jnp.full((chars, 128), -1e30, F32)
        sums = jnp.zeros((chars, 128), F32)
        for h in range(width // 128):
            cols = slice(h * 128, (h + 1) * 128)
            q, k, v = q_ref[rows, cols], k_ref[rows, cols], v_ref[rows, cols]
            zero = jnp.zeros_like(k)
            kk = jnp.concatenate([jnp.where(low, k, zero), jnp.where(low, zero, k)], axis=0)
            vv = jnp.concatenate([jnp.where(low, v, zero), jnp.where(low, zero, v)], axis=0)
            ones = (column == 2 * h + second).astype(F32).astype(BF)
            s = lax.dot_general(q, kk, (((1,), (1,)), ((), ())), preferred_element_type=F32)
            probs = []
            for half in range(2):
                t = jnp.where(seen, s[:, half * chars:(half + 1) * chars], -1e30)
                top = jnp.max(t, axis=-1, keepdims=True)
                tops = jnp.where(key == 2 * h + half, top, tops)
                probs.append(jnp.exp(t - top).astype(BF))
            both = jnp.dot(jnp.concatenate(probs, axis=1), jnp.concatenate([vv, ones], axis=1), preferred_element_type=F32)
            acc_ref[rows, cols] = both[:, :128]
            sums += both[:, 128:]
        top_ref[rows] = tops
        sum_ref[rows] = sums
        for store in stores(b):
            store.start()
        return carry

    lax.fori_loop(0, bars, attend, 0)
    q_store.wait()
    for b in range(bars):
        for store in stores(b):
            store.wait()


def early_decode(gate, normed, pack):
    tokens, width = normed.shape
    hbm = pl.BlockSpec(memory_space=pl.ANY)
    shapes = ((width, BF), (width, F32), (128, F32), (128, F32))
    return pl.pallas_call(
        early_kernel,
        out_shape=[jax.ShapeDtypeStruct((tokens, w), d) for w, d in shapes],
        in_specs=[hbm] * 3,
        out_specs=[hbm] * 4,
        scratch_shapes=[pltpu.VMEM((tokens, w), d) for w, d in shapes]
        + [pltpu.VMEM((tokens, width), BF)] * 3
        + [pltpu.VMEM((3, 128, 8, width), BF), pltpu.SemaphoreType.DMA((4,)), pltpu.SemaphoreType.DMA((13,))],
        compiler_params=pltpu.CompilerParams(vmem_limit_bytes=VMEM_BYTES),
        cost_estimate=pl.CostEstimate(flops=8 << 30, bytes_accessed=16 << 20, transcendentals=1 << 20),
        name="early",
    )(gate, normed, pack)


def late_kernel(*refs):
    pack_ref, out_ref, refs, sources = refs[11], refs[12], refs[13:], refs[:11]
    held, (x_ref, n_ref, c_ref, mid_ref, wk, wo, wup, wdn, sems, loads) = refs[:11], refs[11:]
    parts_ref, ids_ref, prev_ref, len_ref, embed_ref, pos_ref, gain_ref, top_in, sum_in, q_ref, acc_ref = held
    bars, chars = ids_ref.shape
    vocab, width = embed_ref.shape
    copies = [pltpu.make_async_copy(pack_ref.at[:, 1 + j], wk.at[j], sems.at[j]) for j in range(2)]
    copies.append(pltpu.make_async_copy(pack_ref.at[:, 3], wo, sems.at[2]))
    for j in range(4):
        copies.append(pltpu.make_async_copy(pack_ref.at[:, 4 + j], wup.at[j], sems.at[3 + j]))
    for j in range(4):
        rows = pl.ds(32 * j, 32)
        copies.append(pltpu.make_async_copy(pack_ref.at[rows, 8:12], wdn.at[rows], sems.at[7 + j]))
    small = [pltpu.make_async_copy(source, to, loads.at[i]) for i, (source, to) in enumerate(zip(sources, held))]
    for copy in small[:7] + copies[:2]:
        copy.start()
    for copy in small[:7]:
        copy.wait()
    for copy in small[7:]:
        copy.start()
    for b in range(bars):
        x_ref[b * chars:(b + 1) * chars] = embedded(prev_ref[b:b + 1, :], embed_ref, pos_ref)
    vec = jnp.sum(parts_ref[...], axis=0).astype(BF).astype(F32)
    first = vec + pos_ref[0:1].astype(F32)
    normed = rms_rows(first, gain_ref[0:1]).astype(BF)
    kv = []
    for j in range(2):
        copies[j].wait()
        if j == 1:
            copies[2].start()
        kv.append(jnp.dot(normed, wk[j].reshape(width, width), preferred_element_type=F32).astype(BF).astype(F32))
    member = (lax.broadcasted_iota(jnp.int32, (HEADS, width), 1) // 64
              == lax.broadcasted_iota(jnp.int32, (HEADS, width), 0))
    expand = member.astype(BF)

    for copy in small[7:]:
        copy.wait()
    copies[3].start()
    copies[7].start()

    def widen(v):
        high = v.astype(BF)
        rest = (v - high.astype(F32)).astype(BF)
        both = jnp.concatenate([high, rest], axis=1)
        return jnp.dot(both, jnp.concatenate([expand, expand], axis=0), preferred_element_type=F32)

    for b in range(bars):
        rows = slice(b * chars, (b + 1) * chars)
        key = jnp.where(member, kv[0][b:b + 1], 0.0).astype(BF)
        score = lax.dot_general(q_ref[rows, :], key, (((1,), (1,)), ((), ())), preferred_element_type=F32)
        start = lax.broadcasted_iota(jnp.int32, (chars, HEADS), 0) == 0
        before = jnp.where(start, -1e30, top_in[rows, :HEADS])
        score = jnp.where(start, 0.0, score)
        top = jnp.maximum(before, score)
        old = jnp.exp(before - top)
        new = jnp.exp(score - top)
        inverse = 1.0 / (old * sum_in[rows, :HEADS] + new)
        mixed = acc_ref[rows, :] * widen(old * inverse) + kv[1][b:b + 1] * widen(new * inverse)
        c_ref[rows, :] = mixed.astype(BF)
        x_ref[b * chars:b * chars + 1, :] = first[b:b + 1]
    copies[2].wait()
    copies[4].start()
    hidden = x_ref[...] + jnp.dot(c_ref[...], wo[...].reshape(width, width), preferred_element_type=F32)
    x_ref[...] = hidden
    n_ref[...] = rms_rows(hidden, gain_ref[1:2]).astype(BF)
    for j in range(4):
        copies[3 + j].wait()
        if j < 3:
            copies[8 + j].start()
        if j < 2:
            copies[5 + j].start()
        mid_ref[...] = jax.nn.gelu(jnp.dot(n_ref[...], wup[j].reshape(width, width), preferred_element_type=F32)).astype(BF)
        copies[7 + j].wait()
        x_ref[...] += jnp.dot(mid_ref[...], wdn[32 * j:32 * j + 32].reshape(width, width), preferred_element_type=F32)
    last = rms_rows(x_ref[...], gain_ref[2:3]).astype(BF)
    logits = lax.dot_general(embed_ref[...], last, (((1,), (1,)), ((), ())), preferred_element_type=F32)
    top = jnp.max(logits, axis=0, keepdims=True)
    norm = top + jnp.log(jnp.sum(jnp.exp(logits - top), axis=0, keepdims=True))
    for b in range(bars):
        cols = slice(b * chars, (b + 1) * chars)
        hit = lax.broadcasted_iota(jnp.int32, (vocab, chars), 0) == ids_ref[b:b + 1, :]
        picked = jnp.sum(jnp.where(hit, logits[:, cols], 0.0), axis=0, keepdims=True) - norm[:, cols]
        live = lax.broadcasted_iota(jnp.int32, (1, chars), 1) < len_ref[b:b + 1, :]
        out_ref[b:b + 1, :] = jnp.where(live, picked, 0.0)


def late_decode(parts, early, ids, prev, lengths, embed, pos, gain, pack):
    bars, chars = ids.shape
    width = embed.shape[1]
    tokens = bars * chars
    sources = (parts, ids, prev, lengths, embed, pos, gain, early[2], early[3], early[0], early[1])
    t = lambda d: pltpu.VMEM((tokens, width), d)
    return pl.pallas_call(
        late_kernel,
        out_shape=jax.ShapeDtypeStruct((bars, chars), F32),
        in_specs=[pl.BlockSpec(memory_space=pl.ANY)] * 12,
        out_specs=pl.BlockSpec(memory_space=pltpu.VMEM),
        scratch_shapes=[pltpu.VMEM(v.shape, v.dtype) for v in sources] + [t(F32), t(BF), t(BF), t(BF),
                        pltpu.VMEM((2, 128, 8, width), BF), pltpu.VMEM((128, 8, width), BF),
                        pltpu.VMEM((4, 128, 8, width), BF), pltpu.VMEM((128, 4, 8, width), BF),
                        pltpu.SemaphoreType.DMA((11,)), pltpu.SemaphoreType.DMA((11,))],
        compiler_params=pltpu.CompilerParams(vmem_limit_bytes=VMEM_BYTES),
        cost_estimate=pl.CostEstimate(flops=10 << 30, bytes_accessed=24 << 20, transcendentals=4 << 20),
        name="late",
    )(*sources, pack)


def shifted(ids):
    return jnp.concatenate([jnp.full((ids.shape[0], 1), -1, jnp.int32), ids[:, :-1]], axis=1)


GROUP = ("y", "x", "z", "c")


def section_kernel(step, project, x_in, *refs):
    kept = 8 if project else 6 if step == 0 else 5
    weights, refs = refs[:-kept], refs[-kept:]
    if project:
        proj_own, proj_other, out_ref, x_ref, w_ref, sems, p_ref, p_sems = refs
    elif step == 0:
        out_ref, row_ref, x_ref, w_ref, sems, _ = refs
    else:
        out_ref, x_ref, w_ref, sems, row_ref = refs
    blocks, rows, cols = x_ref.shape
    side, depth = cols // 2, blocks * cols
    half = depth // 2
    y, core = lax.axis_index("y"), lax.axis_index("c")
    which = jnp.where(y < 2, (y, 1 - y, 3 - y, 2 + y)[step], (y - 2, y, y - 2, 3 - y)[step])
    chip = lax.axis_index("x") * 4 + lax.axis_index("z")
    load_x = pltpu.make_async_copy(x_in, x_ref, sems.at[4])
    load_x.start()
    held = [(weights[i], weights[i + 1]) for i in range(0, min(len(weights), 6), 2)]
    held += [(weights[6:8], weights[8:])] if len(weights) > 6 else []
    for i, pair in enumerate(held):
        @pl.when(which == i)
        def _():
            for part in range(2):
                span = pl.ds(part * half, half)
                for sem, at in ((0, core), (1, 1 - core)):
                    lanes = pl.ds(pl.multiple_of(at * side, side), side)
                    source = pair[sem].at[span] if i < 3 else pair[sem][part]
                    pltpu.make_async_copy(source, w_ref.at[span, lanes], sems.at[2 * part + sem]).start()
    if project:
        deep = proj_own.shape[0]
        loads = [
            pltpu.make_async_copy(source, p_ref.at[pl.ds(pl.multiple_of(at * deep, deep), deep)], p_sems.at[i])
            for i, (source, at) in enumerate(((proj_own, core), (proj_other, 1 - core)))
        ]
        for load in loads:
            load.start()
    load_x.wait()
    total = jnp.zeros((rows, cols), F32)
    for j in range(blocks):
        v = x_ref[j].astype(F32)
        total += v * v
    scale = lax.rsqrt(jnp.sum(total, axis=-1, keepdims=True) / depth + 1e-05)
    update = jnp.zeros((rows, cols), F32)
    for part in range(2):
        span = pl.ds(part * half, half)
        for sem in range(2):
            at = w_ref.at[span, pl.ds(sem * side, side)]
            pltpu.make_async_copy(weights[0].at[span], at, sems.at[2 * part + sem]).wait()
        wide = jnp.concatenate([x_ref[part * blocks // 2 + j] for j in range(blocks // 2)], axis=1)
        update += jnp.dot(wide, w_ref[span, :], preferred_element_type=F32)
    leaving = (x_ref[chip].astype(F32) + jax.nn.gelu(update * scale)).astype(BF)
    if project:
        for load in loads:
            load.wait()
        partial = jnp.dot(leaving, p_ref[...], preferred_element_type=F32)
        each = rows // blocks
        for j in range(blocks):
            out_ref[j] = partial[j * each:(j + 1) * each]
    elif step == 0:
        out_ref[...] = leaving[:rows // 2]
        row_ref[...] = leaving[rows // 2:]
    else:
        row_ref[...] = leaving
        sends = [pltpu.make_async_copy(row_ref, out_ref.at[j], sems.at[5 + j]) for j in range(blocks)]
        for send in sends:
            send.start()
        for send in sends:
            send.wait()


def section_step(step, x, weights, gate=None, proj=()):
    blocks, rows, cols = x.shape
    vm = pl.BlockSpec(memory_space=pltpu.VMEM)
    hbm = pl.BlockSpec(memory_space=pl.ANY)
    scratch = [pltpu.VMEM(x.shape, BF), pltpu.VMEM((blocks * cols, cols), BF), pltpu.SemaphoreType.DMA((5 + blocks,))]
    if not proj:
        out = [jax.ShapeDtypeStruct((rows // 2, cols), BF)] * 2 if step == 0 else jax.ShapeDtypeStruct(x.shape, BF)
        scratch += [pltpu.VMEM((rows, cols), BF)]
    else:
        width = proj[0].shape[1]
        out = jax.ShapeDtypeStruct((blocks, rows // blocks, width), F32)
        scratch += [pltpu.VMEM((cols, width), BF), pltpu.SemaphoreType.DMA((2,))]
    gates = [] if gate is None else [gate]
    return pl.pallas_call(
        lambda *refs: section_kernel(step, len(proj) > 0, *refs[len(gates):]),
        out_shape=out,
        in_specs=[hbm] * (1 + len(gates) + len(weights) + len(proj)),
        out_specs=[vm, vm] if step == 0 else vm if proj else hbm,
        scratch_shapes=scratch,
        compiler_params=pltpu.CompilerParams(vmem_limit_bytes=VMEM_BYTES),
        cost_estimate=pl.CostEstimate(flops=1, bytes_accessed=1, transcendentals=0),
        name="section",
    )(*gates, x, *weights, *proj)


def prepare_kernel(*refs):
    sources, (bars_in, pack_out, w_out, mine_out, theirs_out), scratch = refs[:6], refs[6:11], refs[11:]
    held, (bars_ref, pack_ref, sems, out_sem) = scratch[:6], scratch[6:]
    a_ref, o_ref, u_ref, d_ref, w_ref, gain_ref = held
    y, core = lax.axis_index("y"), lax.axis_index("c")
    small = fetched(sources[:4] + sources[5:], held[:4] + held[5:], sems)
    rows = [pltpu.make_async_copy(bars_in.at[m], bars_ref.at[i], sems.at[5 + i])
            for i, m in enumerate((jnp.minimum(y, 3 - y), jnp.maximum(y, 3 - y)))]
    depth = w_ref.shape[0]
    spans = [pl.ds(i * depth // 4, depth // 4) for i in range(4)]
    loads = [pltpu.make_async_copy(sources[4].at[span], w_ref.at[span], sems.at[7 + i]) for i, span in enumerate(spans)]
    for load in rows + loads:
        load.start()
    for load in small + rows:
        load.wait()
    width = o_ref.shape[1]
    for i in range(3):
        pack_ref[i] = a_ref[:, i * width:(i + 1) * width]
    pack_ref[3] = o_ref[...]
    for i in range(4):
        pack_ref[4 + i] = u_ref[:, i * width:(i + 1) * width]
        pack_ref[8 + i] = d_ref[8 * i:8 * i + 8]
    store = pltpu.make_async_copy(pack_ref, pack_out, out_sem)
    store.start()
    count = bars_ref.shape[1] // 2
    to = lax.broadcasted_iota(jnp.int32, (count, 2 * count), 0)
    source = lax.broadcasted_iota(jnp.int32, (count, 2 * count), 1)
    for out_ref, at in ((mine_out, core), (theirs_out, 1 - core)):
        pick = (source == to // 4 * 8 + 4 * at + to % 4).astype(F32).astype(BF)
        for i in range(2):
            out_ref[i * count:(i + 1) * count] = jnp.dot(pick, bars_ref[i], preferred_element_type=F32).astype(BF)
    for i in range(gain_ref.shape[0]):
        if i % 8 == 0:
            loads[i // 8].wait()
        span = slice(i * 128, (i + 1) * 128)
        column = jnp.transpose(jnp.broadcast_to(gain_ref[i:i + 1, :], (128, 128)))
        w_out[span, :] = (w_ref[span, :].astype(F32) * column).astype(BF)
    store.wait()


def prepare(bars, *sources):
    width = sources[1].shape[1]
    hbm = pl.BlockSpec(memory_space=pl.ANY)
    vm = pl.BlockSpec(memory_space=pltpu.VMEM)
    rows = jax.ShapeDtypeStruct(bars.shape[1:], BF)
    return pl.pallas_call(
        prepare_kernel,
        out_shape=[jax.ShapeDtypeStruct((12, 8, width), BF), jax.ShapeDtypeStruct(sources[4].shape, BF), rows, rows],
        in_specs=[hbm] * 7,
        out_specs=[hbm, vm, vm, vm],
        scratch_shapes=[pltpu.VMEM(v.shape, v.dtype) for v in sources]
        + [pltpu.VMEM((2,) + bars.shape[1:], BF), pltpu.VMEM((12, 8, width), BF),
           pltpu.SemaphoreType.DMA((11,)), pltpu.SemaphoreType.DMA],
        compiler_params=pltpu.CompilerParams(vmem_limit_bytes=VMEM_BYTES),
        name="prepare",
    )(*sources, bars)


def after_kernel(*refs):
    pass


def after(first, arrays):
    hbm = pl.BlockSpec(memory_space=pl.ANY)
    return pl.pallas_call(
        after_kernel,
        out_shape=[jax.ShapeDtypeStruct(v.shape, v.dtype) for v in arrays],
        in_specs=[hbm] * (len(first) + len(arrays)),
        out_specs=[hbm] * len(arrays),
        input_output_aliases={i + len(first): i for i in range(len(arrays))},
        compiler_params=pltpu.CompilerParams(vmem_limit_bytes=1 << 20),
        cost_estimate=pl.CostEstimate(flops=1, bytes_accessed=1, transcendentals=0),
        name="after",
    )(*first, *arrays)


def body(bar_in, section_weight, section_gain, projection, char_ids, lengths, char_embed, char_pos,
         attn_in, attn_out, ffn_in, ffn_out, norm_gain):
    y, core = lax.axis_index("y"), lax.axis_index("c")
    width = char_embed.shape[1]

    def swap(v):
        return lax.ppermute(v, "c", [(0, 1), (1, 0)])

    def across(v, *pairs):
        return lax.ppermute(v, "y", pairs)

    def ordered(mine, theirs, axis):
        return jnp.where(core == 0, jnp.concatenate([mine, theirs], axis), jnp.concatenate([theirs, mine], axis))

    pack, weight, mine, theirs = prepare(
        bar_in, attn_in, attn_out, ffn_in, ffn_out, section_weight[0], section_gain.reshape(-1, 128))
    pack = lax.all_gather(pack.reshape(96, width), GROUP, axis=0, tiled=True).reshape(128, 12, 8, width)
    theirs = swap(theirs)

    def spread(v):
        return lax.all_to_all(v, ("x", "z"), 0, 0, tiled=True)

    def copies(v):
        return jnp.broadcast_to(v[None], (16,) + v.shape)

    x = spread(copies(ordered(mine, theirs, 1)))
    near, far = after([x], [across(weight, (0, 1), (1, 0), (2, 3), (3, 2)), across(weight, (1, 2), (2, 1), (3, 0))])
    weights = [weight, swap(weight), near, swap(near)]
    half = near.shape[0] // 2
    farther = [across(far[:half], (0, 1), (1, 0), (2, 3)), across(near[half:], (0, 3), (3, 0), (2, 1))]
    far_other = swap(far)
    here, there = section_step(0, x, weights, far_other)
    there = across(there, (0, 3), (1, 2))
    x = spread(copies(jnp.where(y < 2, here, there)))
    farther = after([x], farther)
    weights += [far, far_other, *farther, *[swap(w) for w in farther]]
    normed = embed_chars(shifted(char_ids[0]), char_embed, char_pos, norm_gain)
    x = spread(section_step(1, x, weights))
    x = spread(section_step(2, x, weights))
    out = section_step(3, x, weights, proj=[projection, swap(projection)])
    early = early_decode(out, normed, pack)
    parts = spread(out)
    return late_decode(parts, early, char_ids[0], shifted(char_ids[0]), lengths[0][:, None], char_embed, char_pos, norm_gain, pack)[None]


def solution(mesh):
    fine = jax.sharding.Mesh(mesh.devices.reshape(4, 4, 4, 2), GROUP)
    bar = ("x", "z", "c")
    in_specs = (
        P(None, None, bar),
        P("y", None, bar),
        P("y", None),
        P(bar, None),
        P("y", bar, None),
        P("y", bar),
        P(),
        P(),
        P(GROUP, None),
        P(GROUP, None),
        P(GROUP, None),
        P(GROUP, None),
        P(),
    )
    return jax.shard_map(body, mesh=fine, in_specs=in_specs, out_specs=P("y", bar, None), check_vma=False)
```

```python
import functools
import jax, jax.numpy as jnp
from jax import lax
from jax.sharding import PartitionSpec as P
from jax.experimental import pallas as pl
from jax.experimental.pallas import tpu as pltpu

BF=jnp.bfloat16
F32=jnp.float32

def rms_rows(v, g):
    return v * lax.rsqrt(jnp.mean(v * v, axis=-1, keepdims=True) + 1e-05) * g


HEADS = 16
VMEM_BYTES = 63_000_000


def embedded(prev, embed_ref, pos_ref):
    one_hot = (lax.broadcasted_iota(jnp.int32, (embed_ref.shape[0], prev.shape[1]), 0) == prev).astype(BF)
    rows = lax.dot_general(one_hot, embed_ref[...], (((0,), (0,)), ((), ())), preferred_element_type=F32)
    return rows + pos_ref[...].astype(F32)


def fetched(sources, refs, sems):
    copies = [pltpu.make_async_copy(source, to, sems.at[i]) for i, (source, to) in enumerate(zip(sources, refs))]
    for copy in copies:
        copy.start()
    return copies


def embed_kernel(prev_ref, embed_ref, pos_ref, gain_ref, out_ref):
    bars, chars = prev_ref.shape
    for b in range(bars):
        emb = embedded(prev_ref[b:b + 1, :], embed_ref, pos_ref)
        out_ref[b * chars:(b + 1) * chars] = rms_rows(emb, gain_ref[0:1]).astype(BF)


def embed_chars(prev, embed, pos, gain):
    vm = pl.BlockSpec(memory_space=pltpu.VMEM)
    return pl.pallas_call(
        embed_kernel,
        out_shape=jax.ShapeDtypeStruct((prev.size, embed.shape[1]), BF),
        in_specs=[vm] * 4,
        out_specs=vm,
        compiler_params=pltpu.CompilerParams(vmem_limit_bytes=VMEM_BYTES),
        name="embed",
    )(prev, embed, pos, gain)


def early_kernel(gate_ref, n_in, pack_ref, q_out, acc_out, top_out, sum_out,
                 q_ref, acc_ref, top_ref, sum_ref, n_ref, k_ref, v_ref, wq, sems, out_sems):
    tokens, width = n_ref.shape
    chars = 128
    bars = tokens // chars
    copies = [pltpu.make_async_copy(pack_ref.at[:, j], wq.at[j], sems.at[j]) for j in range(3)]
    load = pltpu.make_async_copy(n_in, n_ref, sems.at[3])
    load.start()
    copies[0].start()
    load.wait()
    q_store = pltpu.make_async_copy(q_ref, q_out, out_sems.at[3 * bars])
    for j, dst in ((0, q_ref), (1, k_ref), (2, v_ref)):
        copies[j].wait()
        if j < 2:
            copies[j + 1].start()
        made = jnp.dot(n_ref[...], wq[j].reshape(width, width), preferred_element_type=F32).astype(BF)
        dst[...] = made * BF(0.125) if j == 0 else made
        if j == 0:
            q_store.start()

    def stores(b):
        rows = pl.ds(b * chars, chars)
        return [pltpu.make_async_copy(source.at[rows], to.at[rows], out_sems.at[3 * b + i])
                for i, (source, to) in enumerate(((acc_ref, acc_out), (top_ref, top_out), (sum_ref, sum_out)))]

    low = lax.broadcasted_iota(jnp.int32, (chars, 128), 1) < 64
    query = lax.broadcasted_iota(jnp.int32, (chars, chars), 0)
    key = lax.broadcasted_iota(jnp.int32, (chars, chars), 1)
    seen = (query >= key) & (key > 0)
    second = lax.broadcasted_iota(jnp.int32, (2 * chars, 128), 0) // chars
    column = lax.broadcasted_iota(jnp.int32, (2 * chars, 128), 1)

    def attend(b, carry):
        rows = pl.ds(b * chars, chars)
        tops = jnp.full((chars, 128), -1e30, F32)
        sums = jnp.zeros((chars, 128), F32)
        for h in range(width // 128):
            cols = slice(h * 128, (h + 1) * 128)
            q, k, v = q_ref[rows, cols], k_ref[rows, cols], v_ref[rows, cols]
            zero = jnp.zeros_like(k)
            kk = jnp.concatenate([jnp.where(low, k, zero), jnp.where(low, zero, k)], axis=0)
            vv = jnp.concatenate([jnp.where(low, v, zero), jnp.where(low, zero, v)], axis=0)
            ones = (column == 2 * h + second).astype(F32).astype(BF)
            s = lax.dot_general(q, kk, (((1,), (1,)), ((), ())), preferred_element_type=F32)
            probs = []
            for half in range(2):
                t = jnp.where(seen, s[:, half * chars:(half + 1) * chars], -1e30)
                top = jnp.max(t, axis=-1, keepdims=True)
                tops = jnp.where(key == 2 * h + half, top, tops)
                probs.append(jnp.exp(t - top).astype(BF))
            both = jnp.dot(jnp.concatenate(probs, axis=1), jnp.concatenate([vv, ones], axis=1), preferred_element_type=F32)
            acc_ref[rows, cols] = both[:, :128]
            sums += both[:, 128:]
        top_ref[rows] = tops
        sum_ref[rows] = sums
        for store in stores(b):
            store.start()
        return carry

    for b in range(bars):
        attend(b, 0)
    q_store.wait()
    for b in range(bars):
        for store in stores(b):
            store.wait()


def early_decode(gate, normed, pack):
    tokens, width = normed.shape
    hbm = pl.BlockSpec(memory_space=pl.ANY)
    shapes = ((width, BF), (width, F32), (128, F32), (128, F32))
    return pl.pallas_call(
        early_kernel,
        out_shape=[jax.ShapeDtypeStruct((tokens, w), d) for w, d in shapes],
        in_specs=[hbm] * 3,
        out_specs=[hbm] * 4,
        scratch_shapes=[pltpu.VMEM((tokens, w), d) for w, d in shapes]
        + [pltpu.VMEM((tokens, width), BF)] * 3
        + [pltpu.VMEM((3, 128, 8, width), BF), pltpu.SemaphoreType.DMA((4,)), pltpu.SemaphoreType.DMA((13,))],
        compiler_params=pltpu.CompilerParams(vmem_limit_bytes=VMEM_BYTES),
        cost_estimate=pl.CostEstimate(flops=8 << 30, bytes_accessed=16 << 20, transcendentals=1 << 20),
        name="early",
    )(gate, normed, pack)


def late_kernel(*refs):
    pack_ref, out_ref, refs, sources = refs[11], refs[12], refs[13:], refs[:11]
    held, (x_ref, n_ref, c_ref, mid_ref, wk, wo, wup, wdn, sems, loads) = refs[:11], refs[11:]
    parts_ref, ids_ref, prev_ref, len_ref, embed_ref, pos_ref, gain_ref, top_in, sum_in, q_ref, acc_ref = held
    bars, chars = ids_ref.shape
    vocab, width = embed_ref.shape
    copies = [pltpu.make_async_copy(pack_ref.at[:, 1 + j], wk.at[j], sems.at[j]) for j in range(2)]
    copies.append(pltpu.make_async_copy(pack_ref.at[:, 3], wo, sems.at[2]))
    for j in range(4):
        copies.append(pltpu.make_async_copy(pack_ref.at[:, 4 + j], wup.at[j], sems.at[3 + j]))
    for j in range(4):
        rows = pl.ds(32 * j, 32)
        copies.append(pltpu.make_async_copy(pack_ref.at[rows, 8:12], wdn.at[rows], sems.at[7 + j]))
    small = [pltpu.make_async_copy(source, to, loads.at[i]) for i, (source, to) in enumerate(zip(sources, held))]
    for copy in small[:7] + copies[:2]:
        copy.start()
    for copy in small[:7]:
        copy.wait()
    for copy in small[7:]:
        copy.start()
    for b in range(bars):
        x_ref[b * chars:(b + 1) * chars] = embedded(prev_ref[b:b + 1, :], embed_ref, pos_ref)
    vec = jnp.sum(parts_ref[...], axis=0).astype(BF).astype(F32)
    first = vec + pos_ref[0:1].astype(F32)
    normed = rms_rows(first, gain_ref[0:1]).astype(BF)
    kv = []
    for j in range(2):
        copies[j].wait()
        if j == 1:
            copies[2].start()
        kv.append(jnp.dot(normed, wk[j].reshape(width, width), preferred_element_type=F32).astype(BF).astype(F32))
    member = (lax.broadcasted_iota(jnp.int32, (HEADS, width), 1) // 64
              == lax.broadcasted_iota(jnp.int32, (HEADS, width), 0))
    expand = member.astype(BF)

    for copy in small[7:]:
        copy.wait()
    copies[3].start()
    copies[7].start()

    def widen(v):
        high = v.astype(BF)
        rest = (v - high.astype(F32)).astype(BF)
        both = jnp.concatenate([high, rest], axis=1)
        return jnp.dot(both, jnp.concatenate([expand, expand], axis=0), preferred_element_type=F32)

    for b in range(bars):
        rows = slice(b * chars, (b + 1) * chars)
        key = jnp.where(member, kv[0][b:b + 1], 0.0).astype(BF)
        score = lax.dot_general(q_ref[rows, :], key, (((1,), (1,)), ((), ())), preferred_element_type=F32)
        start = lax.broadcasted_iota(jnp.int32, (chars, HEADS), 0) == 0
        before = jnp.where(start, -1e30, top_in[rows, :HEADS])
        score = jnp.where(start, 0.0, score)
        top = jnp.maximum(before, score)
        old = jnp.exp(before - top)
        new = jnp.exp(score - top)
        inverse = 1.0 / (old * sum_in[rows, :HEADS] + new)
        mixed = acc_ref[rows, :] * widen(old * inverse) + kv[1][b:b + 1] * widen(new * inverse)
        c_ref[rows, :] = mixed.astype(BF)
        x_ref[b * chars:b * chars + 1, :] = first[b:b + 1]
    copies[2].wait()
    copies[4].start()
    hidden = x_ref[...] + jnp.dot(c_ref[...], wo[...].reshape(width, width), preferred_element_type=F32)
    x_ref[...] = hidden
    n_ref[...] = rms_rows(hidden, gain_ref[1:2]).astype(BF)
    for j in range(4):
        copies[3 + j].wait()
        if j < 3:
            copies[8 + j].start()
        if j < 2:
            copies[5 + j].start()
        made = jnp.dot(n_ref[...], wup[j].reshape(width, width), preferred_element_type=F32)
        mid_ref[:, j % 4 * width:(j % 4 + 1) * width] = jax.nn.gelu(made).astype(BF)
        if j % 4 == 3:
            for i in range(j - 3, j + 1):
                copies[7 + i].wait()
            rows = slice(32 * (j - 3), 32 * j + 32)
            x_ref[...] += jnp.dot(mid_ref[...], wdn[rows].reshape(4 * width, width), preferred_element_type=F32)
    last = rms_rows(x_ref[...], gain_ref[2:3]).astype(BF)
    logits = lax.dot_general(embed_ref[...], last, (((1,), (1,)), ((), ())), preferred_element_type=F32)
    top = jnp.max(logits, axis=0, keepdims=True)
    norm = top + jnp.log(jnp.sum(jnp.exp(logits - top), axis=0, keepdims=True))
    for b in range(bars):
        cols = slice(b * chars, (b + 1) * chars)
        hit = lax.broadcasted_iota(jnp.int32, (vocab, chars), 0) == ids_ref[b:b + 1, :]
        picked = jnp.sum(jnp.where(hit, logits[:, cols], 0.0), axis=0, keepdims=True) - norm[:, cols]
        live = lax.broadcasted_iota(jnp.int32, (1, chars), 1) < len_ref[b:b + 1, :]
        out_ref[b:b + 1, :] = jnp.where(live, picked, 0.0)


def late_decode(parts, early, ids, prev, lengths, embed, pos, gain, pack):
    bars, chars = ids.shape
    width = embed.shape[1]
    tokens = bars * chars
    sources = (parts, ids, prev, lengths, embed, pos, gain, early[2], early[3], early[0], early[1])
    t = lambda d: pltpu.VMEM((tokens, width), d)
    return pl.pallas_call(
        late_kernel,
        out_shape=jax.ShapeDtypeStruct((bars, chars), F32),
        in_specs=[pl.BlockSpec(memory_space=pl.ANY)] * 12,
        out_specs=pl.BlockSpec(memory_space=pltpu.VMEM),
        scratch_shapes=[pltpu.VMEM(v.shape, v.dtype) for v in sources] + [t(F32), t(BF), t(BF), pltpu.VMEM((tokens, 4 * width), BF),
                        pltpu.VMEM((2, 128, 8, width), BF), pltpu.VMEM((128, 8, width), BF),
                        pltpu.VMEM((4, 128, 8, width), BF), pltpu.VMEM((128, 4, 8, width), BF),
                        pltpu.SemaphoreType.DMA((11,)), pltpu.SemaphoreType.DMA((11,))],
        compiler_params=pltpu.CompilerParams(vmem_limit_bytes=VMEM_BYTES),
        cost_estimate=pl.CostEstimate(flops=10 << 30, bytes_accessed=24 << 20, transcendentals=4 << 20),
        name="late",
    )(*sources, pack)


def shifted(ids):
    return jnp.concatenate([jnp.full((ids.shape[0], 1), -1, jnp.int32), ids[:, :-1]], axis=1)


GROUP = ("y", "x", "z", "c")


def section_kernel(step, project, x_in, *refs):
    kept = 8 if project else 6 if step == 0 else 5
    weights, refs = refs[:-kept], refs[-kept:]
    if project:
        proj_own, proj_other, out_ref, x_ref, w_ref, sems, p_ref, p_sems = refs
    elif step == 0:
        out_ref, row_ref, x_ref, w_ref, sems, _ = refs
    else:
        out_ref, x_ref, w_ref, sems, row_ref = refs
    blocks, rows, cols = x_ref.shape
    side, depth = cols // 2, blocks * cols
    half = depth // 2
    y, core = lax.axis_index("y"), lax.axis_index("c")
    which = jnp.where(y < 2, (y, 1 - y, 3 - y, 2 + y)[step], (y - 2, y, y - 2, 3 - y)[step])
    chip = lax.axis_index("x") * 4 + lax.axis_index("z")
    load_x = pltpu.make_async_copy(x_in, x_ref, sems.at[4])
    load_x.start()
    held = [(weights[i], weights[i + 1]) for i in range(0, min(len(weights), 6), 2)]
    held += [(weights[6:8], weights[8:])] if len(weights) > 6 else []
    for i, pair in enumerate(held):
        @pl.when(which == i)
        def _():
            for part in range(2):
                span = pl.ds(part * half, half)
                for sem, at in ((0, core), (1, 1 - core)):
                    lanes = pl.ds(pl.multiple_of(at * side, side), side)
                    source = pair[sem].at[span] if i < 3 else pair[sem][part]
                    pltpu.make_async_copy(source, w_ref.at[span, lanes], sems.at[2 * part + sem]).start()
    if project:
        deep = proj_own.shape[0]
        loads = [
            pltpu.make_async_copy(source, p_ref.at[pl.ds(pl.multiple_of(at * deep, deep), deep)], p_sems.at[i])
            for i, (source, at) in enumerate(((proj_own, core), (proj_other, 1 - core)))
        ]
        for load in loads:
            load.start()
    load_x.wait()
    total = jnp.zeros((rows, cols), F32)
    for j in range(blocks):
        v = x_ref[j].astype(F32)
        total += v * v
    scale = lax.rsqrt(jnp.sum(total, axis=-1, keepdims=True) / depth + 1e-05)
    update = jnp.zeros((rows, cols), F32)
    for part in range(2):
        span = pl.ds(part * half, half)
        for sem in range(2):
            at = w_ref.at[span, pl.ds(sem * side, side)]
            pltpu.make_async_copy(weights[0].at[span], at, sems.at[2 * part + sem]).wait()
        wide = jnp.concatenate([x_ref[part * blocks // 2 + j] for j in range(blocks // 2)], axis=1)
        update += jnp.dot(wide, w_ref[span, :], preferred_element_type=F32)
    leaving = (x_ref[chip].astype(F32) + jax.nn.gelu(update * scale)).astype(BF)
    if project:
        for load in loads:
            load.wait()
        partial = jnp.dot(leaving, p_ref[...], preferred_element_type=F32)
        each = rows // blocks
        for j in range(blocks):
            out_ref[j] = partial[j * each:(j + 1) * each]
    elif step == 0:
        out_ref[...] = leaving[:rows // 2]
        row_ref[...] = leaving[rows // 2:]
    else:
        row_ref[...] = leaving
        sends = [pltpu.make_async_copy(row_ref, out_ref.at[j], sems.at[5 + j]) for j in range(blocks)]
        for send in sends:
            send.start()
        for send in sends:
            send.wait()


def section_step(step, x, weights, gate=None, proj=()):
    blocks, rows, cols = x.shape
    vm = pl.BlockSpec(memory_space=pltpu.VMEM)
    hbm = pl.BlockSpec(memory_space=pl.ANY)
    scratch = [pltpu.VMEM(x.shape, BF), pltpu.VMEM((blocks * cols, cols), BF), pltpu.SemaphoreType.DMA((5 + blocks,))]
    if not proj:
        out = [jax.ShapeDtypeStruct((rows // 2, cols), BF)] * 2 if step == 0 else jax.ShapeDtypeStruct(x.shape, BF)
        scratch += [pltpu.VMEM((rows, cols), BF)]
    else:
        width = proj[0].shape[1]
        out = jax.ShapeDtypeStruct((blocks, rows // blocks, width), F32)
        scratch += [pltpu.VMEM((cols, width), BF), pltpu.SemaphoreType.DMA((2,))]
    gates = [] if gate is None else [gate]
    return pl.pallas_call(
        lambda *refs: section_kernel(step, len(proj) > 0, *refs[len(gates):]),
        out_shape=out,
        in_specs=[hbm] * (1 + len(gates) + len(weights) + len(proj)),
        out_specs=[vm, vm] if step == 0 else vm if proj else hbm,
        scratch_shapes=scratch,
        compiler_params=pltpu.CompilerParams(vmem_limit_bytes=VMEM_BYTES),
        cost_estimate=pl.CostEstimate(flops=1, bytes_accessed=1, transcendentals=0),
        name="section",
    )(*gates, x, *weights, *proj)


def prepare_kernel(*refs):
    sources, (bars_in, pack_out, w_out, mine_out, theirs_out), scratch = refs[:6], refs[6:11], refs[11:]
    held, (bars_ref, pack_ref, sems, out_sem) = scratch[:6], scratch[6:]
    a_ref, o_ref, u_ref, d_ref, w_ref, gain_ref = held
    y, core = lax.axis_index("y"), lax.axis_index("c")
    small = fetched(sources[:4] + sources[5:], held[:4] + held[5:], sems)
    rows = [pltpu.make_async_copy(bars_in.at[m], bars_ref.at[i], sems.at[5 + i])
            for i, m in enumerate((jnp.minimum(y, 3 - y), jnp.maximum(y, 3 - y)))]
    depth = w_ref.shape[0]
    spans = [pl.ds(i * depth // 4, depth // 4) for i in range(4)]
    loads = [pltpu.make_async_copy(sources[4].at[span], w_ref.at[span], sems.at[7 + i]) for i, span in enumerate(spans)]
    for load in rows + loads:
        load.start()
    for load in small + rows:
        load.wait()
    width = o_ref.shape[1]
    for i in range(3):
        pack_ref[i] = a_ref[:, i * width:(i + 1) * width]
    pack_ref[3] = o_ref[...]
    for i in range(4):
        pack_ref[4 + i] = u_ref[:, i * width:(i + 1) * width]
        pack_ref[8 + i] = d_ref[8 * i:8 * i + 8]
    store = pltpu.make_async_copy(pack_ref, pack_out, out_sem)
    store.start()
    count = bars_ref.shape[1] // 2
    to = lax.broadcasted_iota(jnp.int32, (count, 2 * count), 0)
    source = lax.broadcasted_iota(jnp.int32, (count, 2 * count), 1)
    for out_ref, at in ((mine_out, core), (theirs_out, 1 - core)):
        pick = (source == to // 4 * 8 + 4 * at + to % 4).astype(F32).astype(BF)
        for i in range(2):
            out_ref[i * count:(i + 1) * count] = jnp.dot(pick, bars_ref[i], preferred_element_type=F32).astype(BF)
    for i in range(gain_ref.shape[0]):
        if i % 8 == 0:
            loads[i // 8].wait()
        span = slice(i * 128, (i + 1) * 128)
        column = jnp.transpose(jnp.broadcast_to(gain_ref[i:i + 1, :], (128, 128)))
        w_out[span, :] = (w_ref[span, :].astype(F32) * column).astype(BF)
    store.wait()


def prepare(bars, *sources):
    width = sources[1].shape[1]
    hbm = pl.BlockSpec(memory_space=pl.ANY)
    vm = pl.BlockSpec(memory_space=pltpu.VMEM)
    rows = jax.ShapeDtypeStruct(bars.shape[1:], BF)
    return pl.pallas_call(
        prepare_kernel,
        out_shape=[jax.ShapeDtypeStruct((12, 8, width), BF), jax.ShapeDtypeStruct(sources[4].shape, BF), rows, rows],
        in_specs=[hbm] * 7,
        out_specs=[hbm, vm, vm, vm],
        scratch_shapes=[pltpu.VMEM(v.shape, v.dtype) for v in sources]
        + [pltpu.VMEM((2,) + bars.shape[1:], BF), pltpu.VMEM((12, 8, width), BF),
           pltpu.SemaphoreType.DMA((11,)), pltpu.SemaphoreType.DMA],
        compiler_params=pltpu.CompilerParams(vmem_limit_bytes=VMEM_BYTES),
        name="prepare",
    )(*sources, bars)


def after_kernel(*refs):
    pass


def after(first, arrays):
    hbm = pl.BlockSpec(memory_space=pl.ANY)
    return pl.pallas_call(
        after_kernel,
        out_shape=[jax.ShapeDtypeStruct(v.shape, v.dtype) for v in arrays],
        in_specs=[hbm] * (len(first) + len(arrays)),
        out_specs=[hbm] * len(arrays),
        input_output_aliases={i + len(first): i for i in range(len(arrays))},
        compiler_params=pltpu.CompilerParams(vmem_limit_bytes=1 << 20),
        cost_estimate=pl.CostEstimate(flops=1, bytes_accessed=1, transcendentals=0),
        name="after",
    )(*first, *arrays)


def body(bar_in, section_weight, section_gain, projection, char_ids, lengths, char_embed, char_pos,
         attn_in, attn_out, ffn_in, ffn_out, norm_gain):
    y, core = lax.axis_index("y"), lax.axis_index("c")
    width = char_embed.shape[1]

    def swap(v):
        return lax.ppermute(v, "c", [(0, 1), (1, 0)])

    def across(v, *pairs):
        return lax.ppermute(v, "y", pairs)

    def ordered(mine, theirs, axis):
        return jnp.where(core == 0, jnp.concatenate([mine, theirs], axis), jnp.concatenate([theirs, mine], axis))

    pack, weight, mine, theirs = prepare(
        bar_in, attn_in, attn_out, ffn_in, ffn_out, section_weight[0], section_gain.reshape(-1, 128))
    pack = lax.all_gather(pack.reshape(96, width), GROUP, axis=0, tiled=True).reshape(128, 12, 8, width)
    theirs = swap(theirs)

    def spread(v):
        return lax.all_to_all(v, ("x", "z"), 0, 0, tiled=True)

    def copies(v):
        return jnp.broadcast_to(v[None], (16,) + v.shape)

    x = spread(copies(ordered(mine, theirs, 1)))
    near, far = after([x], [across(weight, (0, 1), (1, 0), (2, 3), (3, 2)), across(weight, (1, 2), (2, 1), (3, 0))])
    weights = [weight, swap(weight), near, swap(near)]
    half = near.shape[0] // 2
    farther = [across(far[:half], (0, 1), (1, 0), (2, 3)), across(near[half:], (0, 3), (3, 0), (2, 1))]
    far_other = swap(far)
    here, there = section_step(0, x, weights, far_other)
    there = across(there, (0, 3), (1, 2))
    x = spread(copies(jnp.where(y < 2, here, there)))
    farther = after([x], farther)
    weights += [far, far_other, *farther, *[swap(w) for w in farther]]
    normed = embed_chars(shifted(char_ids[0]), char_embed, char_pos, norm_gain)
    x = spread(section_step(1, x, weights))
    x = spread(section_step(2, x, weights))
    out = section_step(3, x, weights, proj=[projection, swap(projection)])
    early = early_decode(out, normed, pack)
    parts = spread(out)
    return late_decode(parts, early, char_ids[0], shifted(char_ids[0]), lengths[0][:, None], char_embed, char_pos, norm_gain, pack)[None]


def solution(mesh):
    fine = jax.sharding.Mesh(mesh.devices.reshape(4, 4, 4, 2), GROUP)
    bar = ("x", "z", "c")
    in_specs = (
        P(None, None, bar),
        P("y", None, bar),
        P("y", None),
        P(bar, None),
        P("y", bar, None),
        P("y", bar),
        P(),
        P(),
        P(GROUP, None),
        P(GROUP, None),
        P(GROUP, None),
        P(GROUP, None),
        P(),
    )
    return jax.shard_map(body, mesh=fine, in_specs=in_specs, out_specs=P("y", bar, None), check_vma=False)
```
